128 devices in a mesh: sx: 8 (over x_hi, y), sy: 16 (over x_lo, z, core).
Axes of the slice: x: 4 (x_hi: 2, x_lo: 2; x = x_hi * 2 + x_lo), y: 4, z: 4, core: 2. Of those that a mesh axis runs over, the one named last changes fastest.
Arguments:
- query_rows: bfloat16 [32768, 2048], P(('sx', 'sy')), may hold values from -6 to 6
- key_rows: bfloat16 [32768, 2048], P(('sx', 'sy')), may hold values from -6 to 6
- value_rows: bfloat16 [32768, 2048], P(('sx', 'sy')), may hold values from -48 to 48
- cotangent: bfloat16 [32768, 2048], P(('sx', 'sy')), may hold values from -24 to 24
- out_weight: bfloat16 [2048, 2048], replicated, may hold values from -0.125 to 0.125
- sorted_blocks: int32 [16, 128], replicated, may hold values from 0 to 127, as said below
- window_start: int32 [16, 128], P(None, ('sx', 'sy')), may hold values from 0 to 61
Outputs:
- layer_output: bfloat16 [32768, 2048], P(('sx', 'sy'))
- grad_queries: bfloat16 [32768, 2048], P(('sx', 'sy'))
- grad_keys: bfloat16 [32768, 2048], P(('sx', 'sy'))
- grad_values: bfloat16 [32768, 2048], P(('sx', 'sy'))
- weight_grad: float32 [2048, 2048], P(('sx', 'sy'))
The draws below stay inside these ranges and needn't reach their ends.
Inputs may be any that keep to these rules, and one draw needn't show every extreme that they name: `sorted_blocks`: block j lies on the device at position j // 1 in sequence order (sx index outer, sy index inner). For each device, the 16 pairs (h, i) of its own query blocks i name blocks on devices of each sx index exactly 2 times. For any device s and any sy index c, at most 2 pairs (h, i) whose block i lies on a device of sy index c name a block on s, and in every draw some s and c reach 2.
All inputs are finite; a program needn't handle non-finite values.
Results may differ from the reference program's by a relative error of at most 0.025.
Values may be sent and summed in bfloat16 or wider, within the bound.
A program may use at most 128 MiB of HBM per device.

```python
import math
import jax
import jax.numpy as jnp
from jax import lax

HEADS = 16
DH = 128
MODEL = 2048
BLOCK = 256
QB = 1
HD = 2048
NB = 128
TOKENS = 32768
PER_SX = 2
CAP1 = 2


def random_order(subkey, shape):
    width_count = shape[-1]
    scores = jax.random.randint(subkey, shape, 0, 1 << 20) * width_count + jnp.arange(width_count, dtype=jnp.int32)
    return jnp.argsort(scores, axis=-1).astype(jnp.int32)


def draw_sorted_blocks(key, part):
    requests = HEADS * QB
    outer_count = requests // PER_SX
    devices = NB // QB
    inner_count = devices // outer_count
    spare_slots = (inner_count - 1) * CAP1
    subkeys = jax.random.split(key, 5)
    order_ids = random_order(subkeys[0], (devices, requests))
    source_outer = order_ids // PER_SX
    rank_ids = order_ids % PER_SX
    device_ids = jnp.arange(devices, dtype=jnp.int32)
    column = (device_ids // inner_count)[:, None] * PER_SX + rank_ids
    placing = random_order(subkeys[1], (outer_count, inner_count, requests))
    others = random_order(subkeys[2], (outer_count, inner_count, spare_slots))
    hot_inner = jax.random.randint(subkeys[3], (outer_count, inner_count), 0, inner_count)
    later_ids = jnp.clip(placing - CAP1, 0, spare_slots - 1)
    other_inner = jnp.take_along_axis(others, later_ids, axis=-1) // CAP1
    other_inner = other_inner + (other_inner >= hot_inner[:, :, None]).astype(jnp.int32)
    chosen = jnp.where(placing < CAP1, hot_inner[:, :, None], other_inner)
    source_inner = chosen[source_outer, (device_ids % inner_count)[:, None], column]
    local_ids = jax.random.randint(subkeys[4], (devices, requests), 0, QB)
    block_ids = (source_outer * inner_count + source_inner) * QB + local_ids
    return block_ids.reshape(devices, HEADS, QB).transpose(1, 0, 2).reshape(HEADS, NB).astype(jnp.int32)


def draw_query_rows(key, part):
    return jnp.clip(jax.random.normal(jax.random.fold_in(key, 1), (TOKENS, HD), jnp.float32), -6.0, 6.0).astype(jnp.bfloat16)


def draw_key_rows(key, part):
    return jnp.clip(jax.random.normal(jax.random.fold_in(key, 2), (TOKENS, HD), jnp.float32), -6.0, 6.0).astype(jnp.bfloat16)


def place_ends(values, key, smallest, top_value):
    extent = values.shape
    place = [jax.random.randint(jax.random.fold_in(key, axis), (), 0, extent[axis]) for axis in range(len(extent))]
    values = values.at[tuple(place)].set(smallest)
    longest = extent.index(max(extent))
    place[longest] = (place[longest] + 1) % extent[longest]
    return values.at[tuple(place)].set(top_value)


def shard_levels(key, extent, cuts, smallest, top_value):
    def one(dim, parts):
        draws = jax.random.uniform(jax.random.fold_in(jax.random.fold_in(key, 6), dim), (parts,), jnp.float32, smallest / len(cuts), top_value / len(cuts))
        return jnp.repeat(jnp.exp(draws), extent[dim] // parts).reshape((-1,) + (1,) * (len(extent) - dim - 1))

    loudness = one(*cuts[0])
    for cut in cuts[1:]:
        loudness = loudness * one(*cut)
    return loudness


def noise(key, shape, deviation, reach, shards=(), kind=jnp.bfloat16):
    factor_of = shard_levels(key, shape, shards, -0.22, 0.18) if shards else 1.0
    entries = jax.random.normal(key, shape, jnp.float32) * deviation * factor_of
    return jnp.minimum(jnp.maximum(entries, -reach), reach).astype(kind)


def setup_inputs(seed: int = 0) -> dict:
    key_list = jax.random.split(jax.random.key(seed), 8)
    query_rows = draw_query_rows(jax.random.fold_in(key_list[7], 71), 0)
    key_rows = draw_key_rows(jax.random.fold_in(key_list[7], 71), 0)
    value_rows = noise(key_list[2], (TOKENS, HD), 8.0, 48.0, ((0, 128),))
    cotangent = noise(key_list[3], (TOKENS, MODEL), 4.0, 24.0, ((0, 128),))
    out_weight = noise(key_list[4], (HD, MODEL), HD ** -0.5, 0.125)
    sorted_blocks = draw_sorted_blocks(jax.random.fold_in(key_list[7], 71), 0)
    window_start = place_ends(jax.random.randint(key_list[6], (HEADS, NB), 0, BLOCK // 4 - 2), jax.random.fold_in(key_list[6], 1), 0, (BLOCK // 4 - 2) - 1).astype(jnp.int32)
    return {"query_rows": query_rows, "key_rows": key_rows, "value_rows": value_rows, "cotangent": cotangent, "out_weight": out_weight, "sorted_blocks": sorted_blocks, "window_start": window_start}


def head_pass(query_head, key_head, value_head, grad_head, order_ids, start_ids):
    score_scale = 1.0 / math.sqrt(DH)
    group_width = min(NB, 32)
    group_steps = NB // group_width
    key_spots = jnp.arange(BLOCK, dtype=jnp.int32)

    def visit(sums_carry, step_id):
        key_sum, value_sum = sums_carry
        block_ids = (step_id * group_width + jnp.arange(group_width, dtype=jnp.int32)).astype(jnp.int32)
        picked = order_ids[block_ids].astype(jnp.int32)
        query_part = query_head[block_ids].astype(jnp.float32)
        grad_part = grad_head[block_ids].astype(jnp.float32)
        key_set = jnp.concatenate([key_head[block_ids], key_head[picked]], axis=1).astype(jnp.float32)
        value_set = jnp.concatenate([value_head[block_ids], value_head[picked]], axis=1).astype(jnp.float32)
        key_seen = jnp.concatenate([key_spots[None, :] >= start_ids[block_ids][:, None], jnp.ones((group_width, BLOCK), jnp.bool_)], axis=1)
        scores = jnp.einsum('nqd,nkd->nqk', query_part, key_set) * score_scale
        scores = jnp.where(key_seen[:, None, :], scores, -jnp.inf)
        row_max = lax.optimization_barrier(jnp.max(scores, axis=-1, keepdims=True))
        exp_scores = jnp.exp(scores - row_max)
        soft_weights = exp_scores / lax.optimization_barrier(jnp.sum(exp_scores, axis=-1, keepdims=True))
        weights_b = lax.optimization_barrier(soft_weights.astype(jnp.bfloat16)).astype(jnp.float32)
        attended = jnp.einsum('nqk,nkd->nqd', weights_b, value_set).astype(jnp.bfloat16)
        attended_f = lax.optimization_barrier(attended).astype(jnp.float32)
        row_delta = lax.optimization_barrier(jnp.sum(grad_part * attended_f, axis=-1, keepdims=True))
        prob_grad = jnp.einsum('nqd,nkd->nqk', grad_part, value_set)
        dscore = lax.optimization_barrier((soft_weights * (prob_grad - row_delta)).astype(jnp.bfloat16)).astype(jnp.float32)
        grad_query = (jnp.einsum('nqk,nkd->nqd', dscore, key_set) * score_scale).astype(jnp.bfloat16)
        key_terms = jnp.einsum('nqk,nqd->nkd', dscore, query_part) * score_scale
        value_terms = jnp.einsum('nqk,nqd->nkd', weights_b, grad_part)
        sorted_keys = lax.optimization_barrier(key_terms[:, BLOCK:].astype(jnp.bfloat16)).astype(jnp.float32)
        sorted_values = lax.optimization_barrier(value_terms[:, BLOCK:].astype(jnp.bfloat16)).astype(jnp.float32)
        key_sum = key_sum.at[block_ids].add(key_terms[:, :BLOCK]).at[picked].add(sorted_keys)
        value_sum = value_sum.at[block_ids].add(value_terms[:, :BLOCK]).at[picked].add(sorted_values)
        return ((key_sum, value_sum), (attended, grad_query))
    zero_sums = jnp.zeros((NB, BLOCK, DH), jnp.float32)
    (key_sum, value_sum), (attended, grad_query) = lax.scan(visit, (zero_sums, zero_sums), jnp.arange(group_steps, dtype=jnp.int32))
    return (attended.reshape(NB, BLOCK, DH), grad_query.reshape(NB, BLOCK, DH), key_sum.astype(jnp.bfloat16), value_sum.astype(jnp.bfloat16))

def heads_first(matrix):
    return matrix.reshape(NB, BLOCK, HEADS, DH).transpose(2, 0, 1, 3)

def tokens_first(stacked):
    return stacked.transpose(1, 2, 0, 3).reshape(TOKENS, HD)

def per_head(items):
    return head_pass(items[0], items[1], items[2], items[3], items[4], items[5])

def reference(query_rows, key_rows, value_rows, cotangent, out_weight, sorted_blocks, window_start):
    attention_grad = jnp.dot(cotangent, out_weight.T, preferred_element_type=jnp.float32).astype(jnp.bfloat16)
    attended, grad_query, grad_key, grad_value = lax.map(per_head, (heads_first(query_rows), heads_first(key_rows), heads_first(value_rows), heads_first(attention_grad), sorted_blocks, window_start))
    attention = tokens_first(attended)
    layer_output = jnp.dot(attention, out_weight, preferred_element_type=jnp.float32).astype(jnp.bfloat16)
    weight_grad = jnp.dot(attention.T, cotangent, preferred_element_type=jnp.float32) * (1.0 / math.sqrt(TOKENS))
    return (layer_output, tokens_first(grad_query), tokens_first(grad_key), tokens_first(grad_value), weight_grad)
```

```python
import math

import jax
import jax.numpy as jnp
from jax import lax
from jax.experimental import pallas as pl
from jax.experimental.pallas import tpu as pltpu
from jax.sharding import PartitionSpec as P

HEADS = 16
DH = 128
BLOCK = 256
DIM = 2048
PARTS = 8
HALF = PARTS // 2
ROWS = BLOCK // HALF
AHEAD = 2
SCALE = 1.0 / math.sqrt(DH)
MESH = pl.DeviceIdType.MESH
STREAMS = ((0, 1024, "yzx"), (1024, 512, "xyz"), (1536, 512, "zxy"))
VMEM = pl.BlockSpec(memory_space=pltpu.VMEM)
SMEM = pl.BlockSpec(memory_space=pltpu.SMEM)
ANY = pl.BlockSpec(memory_space=pl.ANY)
NT = (((1,), (1,)), ((), ()))
TN = (((0,), (0,)), ((), ()))
F32 = jnp.float32
BF16 = jnp.bfloat16
T_OUT, T_X, T_BACK, T_Y, T_SLOT, T_HEAD, T_USED = 0, 32, 64, 96, 128, 160, 192


def here():
    outer = lax.axis_index("sx")
    inner = lax.axis_index("sy")
    return (outer // 4) * 2 + inner // 8, outer % 4, (inner // 2) % 4, inner % 2


def place(x, y, z, k):
    return {"sx": (x // 2) * 4 + y, "sy": (x % 2) * 8 + z * 2 + k}


def step_x(pos, d):
    return place((pos[0] + d) % 4, pos[1], pos[2], pos[3])


def step_y(pos, d):
    return place(pos[0], (pos[1] + d) % 4, pos[2], pos[3])


def step_z(pos, dz, dk):
    return place(pos[0], pos[1], (pos[2] + dz) % 4, (pos[3] + dk) % 2)


def greet(pos):
    barrier = pltpu.get_barrier_semaphore()
    peers = [step_x(pos, d) for d in (1, 2, 3)] + [step_y(pos, d) for d in (1, 2, 3)]
    peers += [step_z(pos, j // 2, j % 2) for j in range(1, 8)]
    for peer in peers:
        pl.semaphore_signal(barrier, inc=1, device_id=peer, device_id_type=MESH)
    pl.semaphore_wait(barrier, len(peers))


def send(src, dst, send_sem, recv_sem, peer):
    pltpu.make_async_remote_copy(
        src_ref=src,
        dst_ref=dst,
        send_sem=send_sem,
        recv_sem=recv_sem,
        device_id=peer,
        device_id_type=MESH,
    ).start()


def settle(ref, sem):
    pltpu.make_async_copy(ref, ref, sem).wait()


def table_kernel(src_ref, out_ref):
    x, y, z, k = here()
    device = lax.axis_index("sx") * 16 + lax.axis_index("sy")
    src = src_ref[...]
    head = lax.broadcasted_iota(jnp.int32, src.shape, 0)
    target = lax.broadcasted_iota(jnp.int32, src.shape, 1)
    outer = src >> 4
    nth = jnp.zeros_like(src)
    for h in range(HEADS):
        nth += jnp.where((outer[h : h + 1] == outer) & (head > h), 1, 0)
    rank = jnp.zeros_like(src)
    for d in range(8):
        turned = pltpu.roll(src, 16 * d, axis=1) if d else src
        for h in range(HEADS):
            first = head > h
            if d:
                first = first | ((head == h) & (target >= 16 * d))
            rank += jnp.where((turned[h : h + 1] == src) & first, 1, 0)
    tx = (target >> 6) * 2 + ((target >> 3) & 1)
    ty, tz, tk = (target >> 4) & 3, (target >> 1) & 3, target & 1
    sx = (src >> 6) * 2 + ((src >> 3) & 1)
    sy, sz, sk = (src >> 4) & 3, (src >> 1) & 3, src & 1
    column = (tz == z) & (tk == k)
    to_slot = (tx & 1) * 2 + rank
    out_slot = (((tz - z) & 3) * 2 + (tk ^ k)) * 4 + to_slot
    in_slot = (((z - sz) & 3) * 2 + (k ^ sk)) * 4 + to_slot
    x_slot = ((tx - x) & 3) * 8 + ((ty - y) & 3) * 2 + nth
    passing = column & ((src >> 3) == (device >> 3))
    y_slot = ((ty - y) & 3) * 4 + (sx >> 1) * 2 + nth
    y_from = ((x - sx) & 3) * 8 + ((ty - y) & 3) * 2 + nth
    handing = column & (tx == x) & (sy == y)
    mine = target == device
    my_slot = ((y - sy) & 3) * 4 + (sx >> 1) * 2 + nth
    entries = lax.broadcasted_iota(jnp.int32, (32, 128), 0)
    sums = []
    for chosen, spot, value in (
        (src == device, out_slot, head),
        (passing, x_slot, in_slot),
        (passing, in_slot, x_slot),
        (handing, y_slot, y_from),
        (mine, head, my_slot),
        (mine, my_slot, head),
        (src == device, out_slot, head + 1),
    ):
        spot = jnp.where(chosen, spot, -1)
        total = jnp.zeros((32, 128), jnp.int32)
        for h in range(HEADS):
            total += jnp.where(spot[h : h + 1] == entries, value[h : h + 1], 0)
        sums.append(total.astype(F32))
    sums.append(jnp.zeros((32, 128), F32))
    rows = lax.dot_general(
        jnp.ones((8, 128), F32), jnp.concatenate(sums, axis=0), NT, preferred_element_type=F32
    )
    out_ref[...] = rows.astype(jnp.int32)


def make_tables(sorted_blocks):
    return pl.pallas_call(
        table_kernel,
        out_shape=jax.ShapeDtypeStruct((8, 256), jnp.int32),
        in_specs=[VMEM],
        out_specs=VMEM,
    )(sorted_blocks)


def fetch_kernel(
    tab, key, value, cot, weight, landed, grad, cot_other, *scratch
):
    zr, xr, scratch = scratch[:PARTS], scratch[PARTS : 2 * PARTS], scratch[2 * PARTS :]
    wbuf, kv, zs, xs, ys, zss, zrs, xss, xrs, yss, yrs, ysl, cs, cr, wsem = scratch
    pos = here()
    load_w = pltpu.make_async_copy(weight, wbuf, wsem)
    load_w.start()

    def gather_z(p):
        ref = key if p < HALF else value
        rows = pl.ds((p % HALF) * ROWS, ROWS)

        for h in range(HEADS):
            kv[p, h] = ref[rows, h * DH : (h + 1) * DH]

        def piece(n):
            return kv[p, tab[0, T_OUT + n]]

        def own(n, _):
            zr[p][n] = piece(n)
            return _

        def other(n, _):
            zs[p, n - 4] = piece(n)
            return _

        lax.fori_loop(0, 4, own, 0)
        lax.fori_loop(4, 32, other, 0)

    def send_z(p):
        for j in range(1, 8):
            send(
                zs.at[p, pl.ds((j - 1) * 4, 4)], zr[p].at[pl.ds(j * 4, 4)],
                zss.at[p], zrs.at[p], step_z(pos, j // 2, j % 2),
            )

    def pass_x(p):
        settle(zr[p].at[pl.ds(4, 28)], zrs.at[p])

        def own(n, _):
            xr[p][n] = zr[p][tab[0, T_X + n]]
            return _

        def other(n, _):
            xs[p, n - 8] = zr[p][tab[0, T_X + n]]
            return _

        lax.fori_loop(8, 32, other, 0)
        for d in range(1, 4):
            send(
                xs.at[p, pl.ds((d - 1) * 8, 8)], xr[p].at[pl.ds(d * 8, 8)],
                xss.at[p], xrs.at[p], step_x(pos, d),
            )
        lax.fori_loop(0, 8, own, 0)

    def pass_y(p):
        settle(xr[p].at[pl.ds(8, 24)], xrs.at[p])

        def each(n, _):
            ys[p, n] = xr[p][tab[0, T_Y + n]]
            return _

        lax.fori_loop(0, 16, each, 0)
        for d in range(1, 4):
            send(
                ys.at[p, pl.ds(d * 4, 4)], landed.at[p, pl.ds(d * 4, 4)],
                yss.at[p], yrs.at[p], step_y(pos, d),
            )
        pltpu.make_async_copy(
            ys.at[p, pl.ds(0, 4)], landed.at[p, pl.ds(0, 4)], ysl.at[p]
        ).start()

    gather_z(0)
    greet(pos)
    send_z(0)
    for p in range(1, AHEAD):
        gather_z(p)
        send_z(p)
    send(cot, cot_other, cs, cr, step_z(pos, 0, 1))
    for p in range(AHEAD, PARTS):
        gather_z(p)
    load_w.wait()

    def grad_tile(c, _):
        cols = pl.ds(pl.multiple_of(c * 256, 256), 256)
        grad[:, cols] = lax.dot_general(
            cot[...], wbuf[cols, :], NT, preferred_element_type=F32
        ).astype(BF16)
        return _

    lax.fori_loop(0, 8, grad_tile, 0)
    for p in range(PARTS):
        pass_x(p)
        if p + AHEAD < PARTS:
            send_z(p + AHEAD)
        if p >= 1:
            pass_y(p - 1)
    pass_y(PARTS - 1)
    for p in range(PARTS):
        settle(landed.at[p, pl.ds(4, 12)], yrs.at[p])
        settle(landed.at[p, pl.ds(0, 4)], ysl.at[p])
        settle(zs.at[p], zss.at[p])
        settle(xs.at[p], xss.at[p])
        settle(ys.at[p, pl.ds(4, 12)], yss.at[p])
    settle(cot_other, cr)
    settle(cot, cs)


def fetch(tab, key, value, cot, weight):
    slot = (ROWS, DH)
    sems = [pltpu.SemaphoreType.DMA((PARTS,))] * 7 + [pltpu.SemaphoreType.DMA] * 3
    return pl.pallas_call(
        fetch_kernel,
        out_shape=(
            jax.ShapeDtypeStruct((PARTS, 16, *slot), BF16),
            jax.ShapeDtypeStruct((BLOCK, DIM), BF16),
            jax.ShapeDtypeStruct((BLOCK, DIM), BF16),
        ),
        in_specs=[SMEM, VMEM, VMEM, VMEM, ANY],
        out_specs=(VMEM, VMEM, VMEM),
        scratch_shapes=[
            *[pltpu.VMEM((32, *slot), BF16)] * (2 * PARTS),
            pltpu.VMEM((DIM, DIM), BF16),
            pltpu.VMEM((PARTS, HEADS, *slot), BF16),
            pltpu.VMEM((PARTS, 28, *slot), BF16),
            pltpu.VMEM((PARTS, 24, *slot), BF16),
            pltpu.VMEM((PARTS, 16, *slot), BF16),
            *sems,
        ],
        compiler_params=pltpu.CompilerParams(
            collective_id=0, has_side_effects=True, vmem_limit_bytes=58 << 20
        ),
        name="fetch",
    )(tab, key, value, cot, weight)


def attend_kernel(
    tab, start, query, key, value, grad, landed,
    att, att_t, grad_q, own_k, own_v, terms,
):
    h = pl.program_id(0)
    q, g = query[...], grad[...]
    keys = jnp.concatenate([key[...], landed[:HALF, 0].reshape(BLOCK, DH)], axis=0)
    values = jnp.concatenate([value[...], landed[HALF:, 0].reshape(BLOCK, DH)], axis=0)
    scores = lax.dot_general(q, keys, NT, preferred_element_type=F32) * SCALE
    spot = lax.broadcasted_iota(jnp.int32, scores.shape, 1)
    seen = (spot >= BLOCK) | (spot >= start[h, 0])
    scores = jnp.where(seen, scores, -jnp.inf)
    e = jnp.exp(scores - jnp.max(scores, axis=1, keepdims=True))
    probs = e * (1.0 / jnp.sum(e, axis=1, keepdims=True))
    probs_b = probs.astype(BF16)
    a32 = jnp.dot(probs_b, values, preferred_element_type=F32)
    a = a32.astype(BF16)
    att[...] = a
    att_t[...] = a.astype(F32).T.astype(BF16).reshape(1, 4, 2, 16, BLOCK)
    delta = jnp.sum(g.astype(F32) * a.astype(F32), axis=1, keepdims=True)
    pg = lax.dot_general(g, values, NT, preferred_element_type=F32)
    ds = (probs * (pg - delta)).astype(BF16)
    grad_q[...] = (jnp.dot(ds, keys, preferred_element_type=F32) * SCALE).astype(BF16)
    kt = lax.dot_general(ds, q, TN, preferred_element_type=F32) * SCALE
    vt = lax.dot_general(probs_b, g, TN, preferred_element_type=F32)
    own_k[...] = kt[:BLOCK]
    own_v[...] = vt[:BLOCK]
    terms[:HALF, 0] = kt[BLOCK:].astype(BF16).reshape(HALF, ROWS, DH)
    terms[HALF:, 0] = vt[BLOCK:].astype(BF16).reshape(HALF, ROWS, DH)


def attend(tab, start, query, key, value, grad, landed):
    head = pl.BlockSpec((BLOCK, DH), lambda h, tab, start: (0, h))
    slot = pl.BlockSpec(
        (PARTS, 1, ROWS, DH), lambda h, tab, start: (0, tab[0, T_SLOT + h], 0, 0)
    )
    turned = pl.BlockSpec((1, 4, 2, 16, BLOCK), lambda h, tab, start: (h, 0, 0, 0, 0))
    return pl.pallas_call(
        attend_kernel,
        out_shape=(
            jax.ShapeDtypeStruct((BLOCK, DIM), BF16),
            jax.ShapeDtypeStruct((HEADS, 4, 2, 16, BLOCK), BF16),
            jax.ShapeDtypeStruct((BLOCK, DIM), BF16),
            jax.ShapeDtypeStruct((BLOCK, DIM), F32),
            jax.ShapeDtypeStruct((BLOCK, DIM), F32),
            jax.ShapeDtypeStruct((PARTS, 16, ROWS, DH), BF16),
        ),
        grid_spec=pltpu.PrefetchScalarGridSpec(
            num_scalar_prefetch=2,
            grid=(HEADS,),
            in_specs=[head, head, head, head, slot],
            out_specs=[head, turned, head, head, head, slot],
        ),
        compiler_params=pltpu.CompilerParams(vmem_limit_bytes=40 << 20),
        name="attend",
    )(tab, start, query, key, value, grad, landed)


AXES = "xyz"


def pick(order, axis, index):
    spot = [slice(None)] * 5
    spot[order.index(axis)] = index
    return tuple(spot[: len(order)])


def return_kernel(
    tab, terms, att, att_t, cot, cot_other, weight,
    back, layer, wgrad, *scratch,
):
    xb, scratch = scratch[:PARTS], scratch[PARTS:]
    (
    wbuf, at_other, yb, zs, g0, g1, g2, r10, r11, r12, s10, s11, s12,
    r20, r21, r22, s20, s21, s22, r30, r31, r32,
    yss, yrs, ysl, xss, xrs, zss, zrs, zsl, as_, ar, ws, rs, rr,
    ) = scratch
    pos = here()
    coord = dict(zip(AXES, pos[:3]))
    k = pos[3]
    go = {"x": step_x, "y": step_y, "z": lambda pos, d: step_z(pos, d, 0)}
    g, r1, s1 = (g0, g1, g2), (r10, r11, r12), (s10, s11, s12)
    r2, s2, r3 = (r20, r21, r22), (s20, s21, s22), (r30, r31, r32)
    load_w = pltpu.make_async_copy(weight, wbuf, ws)
    load_w.start()
    greet(pos)
    send(att_t.at[:, :, 1 - k], at_other, as_, ar, step_z(pos, 0, 1))
    for p in range(PARTS):
        for d in range(1, 4):
            send(
                terms.at[p, pl.ds(d * 4, 4)], yb.at[p, d], yss.at[p], yrs.at[p],
                step_y(pos, 4 - d),
            )
        pltpu.make_async_copy(terms.at[p, pl.ds(0, 4)], yb.at[p, 0], ysl.at[p]).start()
    settle(at_other, ar)

    for n, (first, width, order) in enumerate(STREAMS):

        def tile(m, c, n=n, first=first):
            cols = pl.ds(pl.multiple_of(first + c * 256, 256), 256)
            mine = att_t[pl.ds(m * 4, 4), :, k].reshape(256, BLOCK)
            theirs = at_other[pl.ds(m * 4, 4)].reshape(256, BLOCK)
            t = jnp.dot(mine, cot[:, cols], preferred_element_type=F32)
            t += jnp.dot(theirs, cot_other[:, cols], preferred_element_type=F32)
            t = t.astype(BF16).reshape(4, 4, 16, 256)
            out = pl.ds(pl.multiple_of(c * 256, 256), 256)
            for i in range(4):
                g[n][(m // 2) * 2 + i % 2, (m % 2) * 2 + i // 2, :, :, out] = t[i]

        def tiles(i, _, tile=tile, n=n, first=first):
            tile(i % 4, i // 4)
            return _

        lax.fori_loop(0, 4 * (width // 256), tiles, 0)
        a = order[0]
        for d in range(1, 4):
            send(
                g[n].at[pick(AXES, a, (coord[a] + d) % 4)], r1[n].at[d - 1],
                rs.at[n, 0], rr.at[n, 0], go[a](pos, d),
            )

    def return_x(p):
        settle(yb.at[p, pl.ds(1, 3)], yrs.at[p])
        settle(yb.at[p, 0], ysl.at[p])
        for d in range(4):
            half = ((pos[0] + 4 - d) % 4) // 2
            src = yb.at[p, :, pl.ds(half * 2, 2)]
            if d:
                send(src, xb[p].at[d], xss.at[p], xrs.at[p], step_x(pos, 4 - d))
            else:
                xb[p][0] = yb[p, :, pl.ds(half * 2, 2)]

    def return_z(p):
        settle(xb[p].at[pl.ds(1, 3)], xrs.at[p])

        def each(n, _):
            e = tab[0, T_BACK + n]
            zs[p, n] = xb[p][e // 8, (e // 2) % 4, e % 2]
            return _

        lax.fori_loop(0, 32, each, 0)
        for j in range(1, 8):
            send(
                zs.at[p, pl.ds(j * 4, 4)], back.at[p, pl.ds(j * 4, 4)],
                zss.at[p], zrs.at[p], step_z(pos, 4 - j // 2, j % 2),
            )
        pltpu.make_async_copy(
            zs.at[p, pl.ds(0, 4)], back.at[p, pl.ds(0, 4)], zsl.at[p]
        ).start()

    def sum_one(n):
        order = STREAMS[n][2]
        a = order[0]
        rest = [b for b in AXES if b != a]
        settle(r1[n], rr.at[n, 0])
        settle(r1[n], rs.at[n, 0])

        def each(i, _):
            at = (i // 4, i % 4)
            spot = list(at)
            spot.insert(AXES.index(a), coord[a])
            t = g[n][tuple(spot)].astype(F32)
            for d in range(3):
                t += r1[n][(d, *at)].astype(F32)
            s1[n][at] = t.astype(BF16)
            return _

        lax.fori_loop(0, 16, each, 0)
        b = order[1]
        for d in range(1, 4):
            send(
                s1[n].at[pick(rest, b, (coord[b] + d) % 4)], r2[n].at[d - 1],
                rs.at[n, 1], rr.at[n, 1], go[b](pos, d),
            )

    def sum_two(n):
        order = STREAMS[n][2]
        rest = [b for b in AXES if b != order[0]]
        settle(r2[n], rr.at[n, 1])
        settle(r2[n], rs.at[n, 1])
        b, c = order[1], order[2]
        for i in range(4):
            spot = [i]
            spot.insert(rest.index(b), coord[b])
            t = s1[n][tuple(spot)].astype(F32)
            for d in range(3):
                t += r2[n][d, i].astype(F32)
            s2[n][i] = t.astype(BF16)
        for d in range(1, 4):
            send(
                s2[n].at[(coord[c] + d) % 4], r3[n].at[d - 1],
                rs.at[n, 2], rr.at[n, 2], go[c](pos, d),
            )

    def sum_three(n):
        first, width, order = STREAMS[n]
        settle(r3[n], rr.at[n, 2])
        settle(r3[n], rs.at[n, 2])
        t = s2[n][coord[order[2]]].astype(F32)
        for d in range(3):
            t += r3[n][d].astype(F32)
        wgrad[:, pl.ds(first, width)] = t * (1.0 / math.sqrt(BLOCK * 128))

    load_w.wait()

    def layer_tile(c, _):
        cols = pl.ds(pl.multiple_of(c * 256, 256), 256)
        layer[:, cols] = jnp.dot(
            att[...], wbuf[:, cols], preferred_element_type=F32
        ).astype(BF16)
        return _

    for p in range(PARTS):
        return_x(p)
        if p == 0:
            lax.fori_loop(0, 8, layer_tile, 0)
        if p >= 1:
            return_z(p - 1)
        if p == 4:
            for n in range(3):
                sum_one(n)
        if p == 6:
            for n in range(3):
                sum_two(n)
    return_z(PARTS - 1)
    for n in range(3):
        sum_three(n)
    for p in range(PARTS):
        settle(back.at[p, pl.ds(4, 28)], zrs.at[p])
        settle(back.at[p, pl.ds(0, 4)], zsl.at[p])
        settle(zs.at[p, pl.ds(4, 28)], zss.at[p])
        settle(xb[p].at[pl.ds(1, 3)], xss.at[p])
        settle(yb.at[p, pl.ds(1, 3)], yss.at[p])
    settle(at_other, as_)


def give_back(tab, terms, att, att_t, cot, cot_other, weight):
    slot = (ROWS, DH)
    widths = [w for _, w, _ in STREAMS]
    per_stream = [
        [pltpu.VMEM((*lead, 16, w), BF16) for w in widths]
        for lead in ((4, 4, 4), (3, 4, 4), (4, 4), (3, 4), (4,), (3,))
    ]
    return pl.pallas_call(
        return_kernel,
        out_shape=(
            jax.ShapeDtypeStruct((PARTS, 32, *slot), BF16),
            jax.ShapeDtypeStruct((BLOCK, DIM), BF16),
            jax.ShapeDtypeStruct((16, DIM), F32),
        ),
        in_specs=[SMEM, VMEM, VMEM, VMEM, VMEM, VMEM, ANY],
        out_specs=(VMEM, VMEM, VMEM),
        scratch_shapes=[
            *[pltpu.VMEM((4, 4, 2, *slot), BF16)] * PARTS,
            pltpu.VMEM((DIM, DIM), BF16),
            pltpu.VMEM((HEADS, 4, 16, BLOCK), BF16),
            pltpu.VMEM((PARTS, 4, 4, *slot), BF16),
            pltpu.VMEM((PARTS, 32, *slot), BF16),
            *[buf for level in per_stream for buf in level],
            *[pltpu.SemaphoreType.DMA((PARTS,))] * 8,
            *[pltpu.SemaphoreType.DMA] * 3,
            pltpu.SemaphoreType.DMA((3, 3)),
            pltpu.SemaphoreType.DMA((3, 3)),
        ],
        compiler_params=pltpu.CompilerParams(
            collective_id=1, has_side_effects=True, vmem_limit_bytes=58 << 20
        ),
        name="give_back",
    )(tab, terms, att, att_t, cot, cot_other, weight)


def final_kernel(tab, back_k, back_v, own_k, own_v, grad_k, grad_v, sum_k, sum_v):
    sum_k[...] = own_k[...]
    sum_v[...] = own_v[...]

    def add(n, _):
        h = tab[0, T_USED + n]

        @pl.when(h > 0)
        def _add():
            cols = pl.ds(pl.multiple_of((h - 1) * DH, DH), DH)
            sum_k[:, cols] += back_k[0, n].astype(F32)
            sum_v[:, cols] += back_v[0, n].astype(F32)

        return _

    lax.fori_loop(0, 32, add, 0)
    grad_k[...] = sum_k[...].astype(BF16)
    grad_v[...] = sum_v[...].astype(BF16)


def finish(tab, back, own_k, own_v):
    rows = pl.BlockSpec((ROWS, DIM), lambda p, tab: (p, 0))
    return pl.pallas_call(
        final_kernel,
        out_shape=(
            jax.ShapeDtypeStruct((BLOCK, DIM), BF16),
            jax.ShapeDtypeStruct((BLOCK, DIM), BF16),
        ),
        grid_spec=pltpu.PrefetchScalarGridSpec(
            num_scalar_prefetch=1,
            grid=(HALF,),
            in_specs=[
                pl.BlockSpec((1, 32, ROWS, DH), lambda p, tab: (p, 0, 0, 0)),
                pl.BlockSpec((1, 32, ROWS, DH), lambda p, tab: (p + HALF, 0, 0, 0)),
                rows,
                rows,
            ],
            out_specs=[rows, rows],
            scratch_shapes=[pltpu.VMEM((ROWS, DIM), F32)] * 2,
        ),
        compiler_params=pltpu.CompilerParams(vmem_limit_bytes=40 << 20),
        name="finish",
    )(tab, back, back, own_k, own_v)


def per_device(
    query_rows, key_rows, value_rows, cotangent, out_weight, sorted_blocks, window_start
):
    tab = make_tables(sorted_blocks)
    landed, grad, cot_other = fetch(tab, key_rows, value_rows, cotangent, out_weight)
    att, att_t, grad_q, own_k, own_v, terms = attend(
        tab, window_start, query_rows, key_rows, value_rows, grad, landed
    )
    back, layer, wgrad = give_back(tab, terms, att, att_t, cotangent, cot_other, out_weight)
    grad_k, grad_v = finish(tab, back, own_k, own_v)
    return layer, grad_q, grad_k, grad_v, wgrad


def solution(mesh):
    rows = P(("sx", "sy"), None)
    return jax.shard_map(
        per_device,
        mesh=mesh,
        in_specs=(rows, rows, rows, rows, P(), P(), P(None, ("sx", "sy"))),
        out_specs=(rows, rows, rows, rows, rows),
        check_vma=False,
    )
```

```python
import math

import jax
import jax.numpy as jnp
from jax import lax
from jax.experimental import pallas as pl
from jax.experimental.pallas import tpu as pltpu
from jax.sharding import PartitionSpec as P

HEADS = 16
DH = 128
BLOCK = 256
DIM = 2048
PARTS = 8
HALF = PARTS // 2
ROWS = BLOCK // HALF
AHEAD = 2
UNROLL = 4
TWIN = 4
EARLY = 4
TILES = 8
LATE = 7
WHEN = ((7, 9), (6, 7), (6, 7))
SCALE = 1.0 / math.sqrt(DH)
MESH = pl.DeviceIdType.MESH
STREAMS = ((0, 1024, "yzx"), (1024, 512, "xyz"), (1536, 512, "zxy"))
VMEM = pl.BlockSpec(memory_space=pltpu.VMEM)
SMEM = pl.BlockSpec(memory_space=pltpu.SMEM)
ANY = pl.BlockSpec(memory_space=pl.ANY)
NT = (((1,), (1,)), ((), ()))
TN = (((0,), (0,)), ((), ()))
F32 = jnp.float32
BF16 = jnp.bfloat16
T_OUT, T_X, T_BACK, T_Y, T_SLOT, T_HEAD, T_USED = 0, 32, 64, 96, 128, 160, 192


def here():
    outer = lax.axis_index("sx")
    inner = lax.axis_index("sy")
    return (outer // 4) * 2 + inner // 8, outer % 4, (inner // 2) % 4, inner % 2


def place(x, y, z, k):
    return {"sx": (x // 2) * 4 + y, "sy": (x % 2) * 8 + z * 2 + k}


def step_x(pos, d):
    return place((pos[0] + d) % 4, pos[1], pos[2], pos[3])


def step_y(pos, d):
    return place(pos[0], (pos[1] + d) % 4, pos[2], pos[3])


def step_z(pos, dz, dk):
    return place(pos[0], pos[1], (pos[2] + dz) % 4, (pos[3] + dk) % 2)


def greet(pos):
    barrier = pltpu.get_barrier_semaphore()
    peers = [step_x(pos, d) for d in (1, 2, 3)] + [step_y(pos, d) for d in (1, 2, 3)]
    peers += [step_z(pos, j // 2, j % 2) for j in range(1, 8)]
    for peer in peers:
        pl.semaphore_signal(barrier, inc=1, device_id=peer, device_id_type=MESH)
    pl.semaphore_wait(barrier, len(peers))


def send(src, dst, send_sem, recv_sem, peer):
    pltpu.make_async_remote_copy(
        src_ref=src,
        dst_ref=dst,
        send_sem=send_sem,
        recv_sem=recv_sem,
        device_id=peer,
        device_id_type=MESH,
    ).start()


def settle(ref, sem):
    pltpu.make_async_copy(ref, ref, sem).wait()


def table_kernel(src_ref, out_ref):
    x, y, z, k = here()
    device = lax.axis_index("sx") * 16 + lax.axis_index("sy")
    src = src_ref[...]
    head = lax.broadcasted_iota(jnp.int32, src.shape, 0)
    target = lax.broadcasted_iota(jnp.int32, src.shape, 1)
    outer = src >> 4
    nth = jnp.zeros_like(src)
    for h in range(HEADS):
        nth += jnp.where((outer[h : h + 1] == outer) & (head > h), 1, 0)
    rank = jnp.zeros_like(src)
    for d in range(8):
        turned = pltpu.roll(src, 16 * d, axis=1) if d else src
        for h in range(HEADS):
            first = head > h
            if d:
                first = first | ((head == h) & (target >= 16 * d))
            rank += jnp.where((turned[h : h + 1] == src) & first, 1, 0)
    tx = (target >> 6) * 2 + ((target >> 3) & 1)
    ty, tz, tk = (target >> 4) & 3, (target >> 1) & 3, target & 1
    sx = (src >> 6) * 2 + ((src >> 3) & 1)
    sy, sz, sk = (src >> 4) & 3, (src >> 1) & 3, src & 1
    column = (tz == z) & (tk == k)
    to_slot = (tx & 1) * 2 + rank
    out_slot = (((tz - z) & 3) * 2 + (tk ^ k)) * 4 + to_slot
    in_slot = (((z - sz) & 3) * 2 + (k ^ sk)) * 4 + to_slot
    x_slot = ((tx - x) & 3) * 8 + ((ty - y) & 3) * 2 + nth
    passing = column & ((src >> 3) == (device >> 3))
    y_slot = ((ty - y) & 3) * 4 + (sx >> 1) * 2 + nth
    y_from = ((x - sx) & 3) * 8 + ((ty - y) & 3) * 2 + nth
    handing = column & (tx == x) & (sy == y)
    mine = target == device
    my_slot = ((y - sy) & 3) * 4 + (sx >> 1) * 2 + nth
    entries = lax.broadcasted_iota(jnp.int32, (32, 128), 0)
    sums = []
    for chosen, spot, value in (
        (src == device, out_slot, head),
        (passing, x_slot, in_slot),
        (passing, in_slot, x_slot),
        (handing, y_slot, y_from),
        (mine, head, my_slot),
        (mine, my_slot, head),
        (src == device, out_slot, head + 1),
    ):
        spot = jnp.where(chosen, spot, -1)
        total = jnp.zeros((32, 128), jnp.int32)
        for h in range(HEADS):
            total += jnp.where(spot[h : h + 1] == entries, value[h : h + 1], 0)
        sums.append(total.astype(F32))
    sums.append(jnp.zeros((32, 128), F32))
    rows = lax.dot_general(
        jnp.ones((8, 128), F32), jnp.concatenate(sums, axis=0), NT, preferred_element_type=F32
    )
    out_ref[...] = rows.astype(jnp.int32)


def make_tables(sorted_blocks):
    return pl.pallas_call(
        table_kernel,
        out_shape=jax.ShapeDtypeStruct((8, 256), jnp.int32),
        in_specs=[VMEM],
        out_specs=VMEM,
    )(sorted_blocks)


def fetch_kernel(
    tab, key, value, cot, weight, landed, grad, cot_other, *scratch
):
    zr, xr, scratch = scratch[:PARTS], scratch[PARTS : 2 * PARTS], scratch[2 * PARTS :]
    wbuf, kv, zs, xs, ys, zss, zrs, xss, xrs, yss, yrs, ysl, cs, cr, wsem = scratch
    pos = here()
    load_w = pltpu.make_async_copy(weight, wbuf, wsem)
    load_w.start()

    def gather_z(p):
        ref = key if p < HALF else value
        rows = pl.ds((p % HALF) * ROWS, ROWS)

        for h in range(HEADS):
            kv[p, h] = ref[rows, h * DH : (h + 1) * DH]

        def piece(n):
            return kv[p, tab[0, T_OUT + n]]

        def own(n, _):
            zr[p][n] = piece(n)
            return _

        def other(n, _):
            zs[p, n - 4] = piece(n)
            return _

        lax.fori_loop(0, 4, own, 0, unroll=4)
        lax.fori_loop(4, 32, other, 0, unroll=UNROLL)

    def send_z(p):
        for j in range(1, 8):
            send(
                zs.at[p, pl.ds((j - 1) * 4, 4)], zr[p].at[pl.ds(j * 4, 4)],
                zss.at[p], zrs.at[p], step_z(pos, j // 2, j % 2),
            )

    def pass_x(p):
        settle(zr[p].at[pl.ds(4, 28)], zrs.at[p])

        def own(n, _):
            xr[p][n] = zr[p][tab[0, T_X + n]]
            return _

        def other(n, _):
            xs[p, n - 8] = zr[p][tab[0, T_X + n]]
            return _

        lax.fori_loop(8, 32, other, 0, unroll=UNROLL)
        for d in range(1, 4):
            send(
                xs.at[p, pl.ds((d - 1) * 8, 8)], xr[p].at[pl.ds(d * 8, 8)],
                xss.at[p], xrs.at[p], step_x(pos, d),
            )
        lax.fori_loop(0, 8, own, 0, unroll=UNROLL)

    def pass_y(p):
        settle(xr[p].at[pl.ds(8, 24)], xrs.at[p])

        def each(n, _):
            ys[p, n] = xr[p][tab[0, T_Y + n]]
            return _

        lax.fori_loop(0, 16, each, 0, unroll=UNROLL)
        for d in range(1, 4):
            send(
                ys.at[p, pl.ds(d * 4, 4)], landed.at[p, pl.ds(d * 4, 4)],
                yss.at[p], yrs.at[p], step_y(pos, d),
            )
        pltpu.make_async_copy(
            ys.at[p, pl.ds(0, 4)], landed.at[p, pl.ds(0, 4)], ysl.at[p]
        ).start()

    def grad_tile(c):
        cols = pl.ds(c * 256, 256)
        grad[:, cols] = lax.dot_general(
            cot[...], wbuf[cols, :], NT, preferred_element_type=F32
        ).astype(BF16)

    gather_z(0)
    greet(pos)
    send_z(0)
    for p in range(1, AHEAD):
        gather_z(p)
        send_z(p)
    send(cot, cot_other, cs, cr, step_z(pos, 0, 1))
    for p in range(PARTS):
        if p + AHEAD < PARTS:
            gather_z(p + AHEAD)
            send_z(p + AHEAD)
        pass_x(p)
        if p >= 1:
            pass_y(p - 1)
        if p == 0:
            load_w.wait()
        for c in range(8):
            if c * PARTS // 8 == p:
                grad_tile(c)
    pass_y(PARTS - 1)
    for p in range(PARTS):
        settle(landed.at[p, pl.ds(4, 12)], yrs.at[p])
        settle(landed.at[p, pl.ds(0, 4)], ysl.at[p])
        settle(zs.at[p], zss.at[p])
        settle(xs.at[p], xss.at[p])
        settle(ys.at[p, pl.ds(4, 12)], yss.at[p])
    settle(cot_other, cr)
    settle(cot, cs)


def fetch(tab, key, value, cot, weight):
    slot = (ROWS, DH)
    sems = [pltpu.SemaphoreType.DMA((PARTS,))] * 7 + [pltpu.SemaphoreType.DMA] * 3
    return pl.pallas_call(
        fetch_kernel,
        out_shape=(
            jax.ShapeDtypeStruct((PARTS, 16, *slot), BF16),
            jax.ShapeDtypeStruct((BLOCK, DIM), BF16),
            jax.ShapeDtypeStruct((BLOCK, DIM), BF16),
        ),
        in_specs=[SMEM, VMEM, VMEM, VMEM, ANY],
        out_specs=(VMEM, VMEM, VMEM),
        scratch_shapes=[
            *[pltpu.VMEM((32, *slot), BF16)] * (2 * PARTS),
            pltpu.VMEM((DIM, DIM), BF16),
            pltpu.VMEM((PARTS, HEADS, *slot), BF16),
            pltpu.VMEM((PARTS, 28, *slot), BF16),
            pltpu.VMEM((PARTS, 24, *slot), BF16),
            pltpu.VMEM((PARTS, 16, *slot), BF16),
            *sems,
        ],
        compiler_params=pltpu.CompilerParams(
            collective_id=0, has_side_effects=True, vmem_limit_bytes=58 << 20
        ),
        name="fetch",
    )(tab, key, value, cot, weight)


AXES = "xyz"


def pick(order, axis, index):
    spot = [slice(None)] * 5
    spot[order.index(axis)] = index
    return tuple(spot[: len(order)])


def attend_kernel(
    tab, start, query, key, value, grad, landed, cot_in, cot_other_in, weight,
    back, layer_out, wgrad, grad_q_out, own_k_out, own_v_out, *scratch
):
    xb, scratch = scratch[:PARTS], scratch[PARTS:]
    (
        q_in, k_in, v_in, g_in, f_in, cot, cot_other, wbuf,
        att, att_t, at_other, pbuf, grad_q, own_k, own_v, layer, terms, ys, yb, zs,
        g0, g1, g2, r10, r11, r12, s10, s11, s12, r20, r21, r22, s20, s21, s22, r30, r31, r32,
        yss, yrs, xss, xrs, zss, zrs, zsl, as_, ar, ins, outs, rs, rr,
    ) = scratch
    pos = here()
    coord = dict(zip(AXES, pos[:3]))
    k = pos[3]
    go = {"x": step_x, "y": step_y, "z": lambda pos, d: step_z(pos, d, 0)}
    g, r1, s1 = (g0, g1, g2), (r10, r11, r12), (s10, s11, s12)
    r2, s2, r3 = (r20, r21, r22), (s20, s21, s22), (r30, r31, r32)
    loads = [
        pltpu.make_async_copy(src, dst, ins.at[n])
        for n, (src, dst) in enumerate(
            (
                (query, q_in), (key, k_in), (landed, f_in), (value, v_in), (grad, g_in),
                (cot_in, cot), (cot_other_in, cot_other), (weight, wbuf),
            )
        )
    ]
    for load in loads:
        load.start()
    greet(pos)

    def fetched(h, first):
        slot = tab[0, T_SLOT + h]
        return jnp.concatenate([f_in[p, slot] for p in range(first, first + HALF)], axis=0)

    def forward(h, _):
        cols = pl.ds(pl.multiple_of(h * DH, DH), DH)
        qh = q_in[:, cols]
        own = lax.dot_general(qh, k_in[:, cols], NT, preferred_element_type=F32) * SCALE
        spot = lax.broadcasted_iota(jnp.int32, own.shape, 1)
        own = jnp.where(spot >= start[h, 0], own, -jnp.inf)
        far = lax.dot_general(qh, fetched(h, 0), NT, preferred_element_type=F32) * SCALE
        top = jnp.max(jnp.maximum(own, far), axis=1, keepdims=True)
        own, far = jnp.exp(own - top), jnp.exp(far - top)
        share = 1.0 / jnp.sum(own + far, axis=1, keepdims=True)
        own, far = own * share, far * share
        pbuf[h, 0] = own
        pbuf[h, 1] = far
        a = jnp.dot(own.astype(BF16), v_in[:, cols], preferred_element_type=F32)
        a += jnp.dot(far.astype(BF16), fetched(h, HALF), preferred_element_type=F32)
        a = a.astype(BF16)
        att[:, cols] = a
        att_t[h] = a.astype(F32).T.astype(BF16).reshape(4, 2, 16, BLOCK)
        return _

    def backward(h, _):
        cols = pl.ds(pl.multiple_of(h * DH, DH), DH)
        gh, qh, probs = g_in[:, cols], q_in[:, cols], pbuf[h, 1]
        delta = jnp.sum(gh.astype(F32) * att[:, cols].astype(F32), axis=1, keepdims=True)
        pg = lax.dot_general(gh, fetched(h, HALF), NT, preferred_element_type=F32)
        ds = (probs * (pg - delta)).astype(BF16)
        kt = lax.dot_general(ds, qh, TN, preferred_element_type=F32) * SCALE
        vt = lax.dot_general(probs.astype(BF16), gh, TN, preferred_element_type=F32)
        pbuf[h, 1] = ds.astype(F32)
        for p in range(HALF):
            rows = slice(p * ROWS, (p + 1) * ROWS)
            terms[p, h] = kt[rows].astype(BF16)
            terms[p + HALF, h] = vt[rows].astype(BF16)
        return _

    def backward_own(h, _):
        cols = pl.ds(pl.multiple_of(h * DH, DH), DH)
        gh, qh, kh, probs = g_in[:, cols], q_in[:, cols], k_in[:, cols], pbuf[h, 0]
        delta = jnp.sum(gh.astype(F32) * att[:, cols].astype(F32), axis=1, keepdims=True)
        pg = lax.dot_general(gh, v_in[:, cols], NT, preferred_element_type=F32)
        ds = (probs * (pg - delta)).astype(BF16)
        gq = jnp.dot(ds, kh, preferred_element_type=F32)
        gq += jnp.dot(pbuf[h, 1].astype(BF16), fetched(h, 0), preferred_element_type=F32)
        grad_q[:, cols] = (gq * SCALE).astype(BF16)
        kt = lax.dot_general(ds, qh, TN, preferred_element_type=F32) * SCALE
        vt = lax.dot_general(probs.astype(BF16), gh, TN, preferred_element_type=F32)
        own_k[h] = kt.astype(BF16)
        own_v[h] = vt.astype(BF16)
        return _

    for load in loads[:4]:
        load.wait()
    lax.fori_loop(0, HEADS, forward, 0, unroll=TWIN)
    send(att_t.at[:, :, 1 - k], at_other, as_, ar, step_z(pos, 0, 1))
    for load in loads[4:7]:
        load.wait()
    lax.fori_loop(0, EARLY, backward, 0, unroll=TWIN)
    settle(at_other, ar)

    def partial(n):
        first, width, _ = STREAMS[n]

        def tile(m, c):
            cols = pl.ds(pl.multiple_of(first + c * 256, 256), 256)
            mine = att_t[pl.ds(m * 4, 4), :, k].reshape(256, BLOCK)
            theirs = at_other[pl.ds(m * 4, 4)].reshape(256, BLOCK)
            t = jnp.dot(mine, cot[:, cols], preferred_element_type=F32)
            t += jnp.dot(theirs, cot_other[:, cols], preferred_element_type=F32)
            t = t.astype(BF16).reshape(4, 4, 16, 256)
            out = pl.ds(pl.multiple_of(c * 256, 256), 256)
            for i in range(4):
                g[n][(m // 2) * 2 + i % 2, (m % 2) * 2 + i // 2, :, :, out] = t[i]

        def tiles(i, _):
            tile(i % 4, i // 4)
            return _

        lax.fori_loop(0, 4 * (width // 256), tiles, 0, unroll=TILES)

    def send_one(n):
        a = STREAMS[n][2][0]
        for d in range(1, 4):
            send(
                g[n].at[pick(AXES, a, (coord[a] + d) % 4)], r1[n].at[d - 1],
                rs.at[n, 0], rr.at[n, 0], go[a](pos, d),
            )

    for n in (2, 1):
        partial(n)
        send_one(n)
    lax.fori_loop(EARLY, HEADS, backward, 0, unroll=TWIN)

    def return_y(p):
        def own(n, _):
            yb[p, 0, n] = terms[p, tab[0, T_HEAD + n]]
            return _

        def other(n, _):
            ys[p, n - 4] = terms[p, tab[0, T_HEAD + n]]
            return _

        lax.fori_loop(4, 16, other, 0, unroll=4)
        for d in range(1, 4):
            send(
                ys.at[p, pl.ds(d * 4 - 4, 4)], yb.at[p, d], yss.at[p], yrs.at[p],
                step_y(pos, 4 - d),
            )
        lax.fori_loop(0, 4, own, 0, unroll=4)

    def return_x(p):
        settle(yb.at[p, pl.ds(1, 3)], yrs.at[p])
        for d in range(4):
            half = ((pos[0] + 4 - d) % 4) // 2
            src = yb.at[p, :, pl.ds(half * 2, 2)]
            if d:
                send(src, xb[p].at[d], xss.at[p], xrs.at[p], step_x(pos, 4 - d))
            else:
                xb[p][0] = yb[p, :, pl.ds(half * 2, 2)]

    def return_z(p):
        settle(xb[p].at[pl.ds(1, 3)], xrs.at[p])

        def each(n, _):
            e = tab[0, T_BACK + n]
            zs[p, n] = xb[p][e // 8, (e // 2) % 4, e % 2]
            return _

        lax.fori_loop(0, 32, each, 0, unroll=UNROLL)
        for j in range(1, 8):
            send(
                zs.at[p, pl.ds(j * 4, 4)], back.at[p, pl.ds(j * 4, 4)],
                zss.at[p], zrs.at[p], step_z(pos, 4 - j // 2, j % 2),
            )
        pltpu.make_async_copy(
            zs.at[p, pl.ds(0, 4)], back.at[p, pl.ds(0, 4)], zsl.at[p]
        ).start()

    def sum_one(n):
        order = STREAMS[n][2]
        a = order[0]
        rest = [b for b in AXES if b != a]
        settle(r1[n], rr.at[n, 0])
        settle(r1[n], rs.at[n, 0])

        def each(i, _):
            at = (i // 4, i % 4)
            spot = list(at)
            spot.insert(AXES.index(a), coord[a])
            t = g[n][tuple(spot)].astype(F32)
            for d in range(3):
                t += r1[n][(d, *at)].astype(F32)
            s1[n][at] = t.astype(BF16)
            return _

        lax.fori_loop(0, 16, each, 0)
        b = order[1]
        for d in range(1, 4):
            send(
                s1[n].at[pick(rest, b, (coord[b] + d) % 4)], r2[n].at[d - 1],
                rs.at[n, 1], rr.at[n, 1], go[b](pos, d),
            )

    def sum_two(n):
        order = STREAMS[n][2]
        rest = [b for b in AXES if b != order[0]]
        settle(r2[n], rr.at[n, 1])
        settle(r2[n], rs.at[n, 1])
        b, c = order[1], order[2]
        for i in range(4):
            spot = [i]
            spot.insert(rest.index(b), coord[b])
            t = s1[n][tuple(spot)].astype(F32)
            for d in range(3):
                t += r2[n][d, i].astype(F32)
            s2[n][i] = t.astype(BF16)
        for d in range(1, 4):
            send(
                s2[n].at[(coord[c] + d) % 4], r3[n].at[d - 1],
                rs.at[n, 2], rr.at[n, 2], go[c](pos, d),
            )

    def sum_three(n):
        first, width, order = STREAMS[n]
        settle(r3[n], rr.at[n, 2])
        settle(r3[n], rs.at[n, 2])
        t = s2[n][coord[order[2]]].astype(F32)
        for d in range(3):
            t += r3[n][d].astype(F32)
        wgrad[:, pl.ds(first, width)] = t * (1.0 / math.sqrt(BLOCK * 128))

    def layer_tile(c, _):
        cols = pl.ds(pl.multiple_of(c * 256, 256), 256)
        layer[:, cols] = jnp.dot(
            att[...], wbuf[:, cols], preferred_element_type=F32
        ).astype(BF16)
        return _

    stores = [
        pltpu.make_async_copy(src, dst, outs.at[n])
        for n, (src, dst) in enumerate(
            ((grad_q, grad_q_out), (own_k, own_k_out), (own_v, own_v_out), (layer, layer_out))
        )
    ]
    for p in range(PARTS):
        return_y(p)
        if p == LATE:
            partial(0)
    send_one(0)
    each = HEADS // PARTS
    for p in range(PARTS):
        return_x(p)
        if p >= 1:
            return_z(p - 1)
        if p == 1:
            loads[7].wait()
            lax.fori_loop(0, 8, layer_tile, 0)
            stores[3].start()
        lax.fori_loop(p * each, (p + 1) * each, backward_own, 0, unroll=each)
        for level, step in enumerate((sum_one, sum_two)):
            for n in range(3):
                if WHEN[n][level] == p:
                    step(n)
    for store in stores[:3]:
        store.start()
    return_z(PARTS - 1)
    for n in (1, 2):
        sum_three(n)
    sum_two(0)
    sum_three(0)
    for p in range(PARTS):
        settle(back.at[p, pl.ds(4, 28)], zrs.at[p])
        settle(back.at[p, pl.ds(0, 4)], zsl.at[p])
        settle(zs.at[p, pl.ds(4, 28)], zss.at[p])
        settle(xb[p].at[pl.ds(1, 3)], xss.at[p])
        settle(ys.at[p], yss.at[p])
    settle(at_other, as_)
    for store in stores:
        store.wait()


def attend(tab, start, query, key, value, grad, landed, cot, cot_other, weight):
    slot = (ROWS, DH)
    tokens = (BLOCK, DIM)
    widths = [w for _, w, _ in STREAMS]
    per_stream = [
        [pltpu.VMEM((*lead, 16, w), BF16) for w in widths]
        for lead in ((4, 4, 4), (3, 4, 4), (4, 4), (3, 4), (4,), (3,))
    ]
    return pl.pallas_call(
        attend_kernel,
        out_shape=(
            jax.ShapeDtypeStruct((PARTS, 32, *slot), BF16),
            jax.ShapeDtypeStruct(tokens, BF16),
            jax.ShapeDtypeStruct((16, DIM), F32),
            jax.ShapeDtypeStruct(tokens, BF16),
            jax.ShapeDtypeStruct((HEADS, BLOCK, DH), BF16),
            jax.ShapeDtypeStruct((HEADS, BLOCK, DH), BF16),
        ),
        in_specs=[SMEM, SMEM, *[ANY] * 8],
        out_specs=(ANY, ANY, VMEM, ANY, ANY, ANY),
        scratch_shapes=[
            *[pltpu.VMEM((4, 4, 2, *slot), BF16)] * PARTS,
            *[pltpu.VMEM(tokens, BF16)] * 4,
            pltpu.VMEM((PARTS, 16, *slot), BF16),
            *[pltpu.VMEM(tokens, BF16)] * 2,
            pltpu.VMEM((DIM, DIM), BF16),
            pltpu.VMEM(tokens, BF16),
            pltpu.VMEM((HEADS, 4, 2, 16, BLOCK), BF16),
            pltpu.VMEM((HEADS, 4, 16, BLOCK), BF16),
            pltpu.VMEM((HEADS, 2, BLOCK, BLOCK), F32),
            pltpu.VMEM(tokens, BF16),
            pltpu.VMEM((HEADS, BLOCK, DH), BF16),
            pltpu.VMEM((HEADS, BLOCK, DH), BF16),
            pltpu.VMEM(tokens, BF16),
            pltpu.VMEM((PARTS, 16, *slot), BF16),
            pltpu.VMEM((PARTS, 12, *slot), BF16),
            pltpu.VMEM((PARTS, 4, 4, *slot), BF16),
            pltpu.VMEM((PARTS, 32, *slot), BF16),
            *[buf for level in per_stream for buf in level],
            *[pltpu.SemaphoreType.DMA((PARTS,))] * 7,
            *[pltpu.SemaphoreType.DMA] * 2,
            pltpu.SemaphoreType.DMA((8,)),
            pltpu.SemaphoreType.DMA((4,)),
            pltpu.SemaphoreType.DMA((3, 3)),
            pltpu.SemaphoreType.DMA((3, 3)),
        ],
        compiler_params=pltpu.CompilerParams(
            collective_id=1, has_side_effects=True, vmem_limit_bytes=62 << 20
        ),
        name="attend",
    )(tab, start, query, key, value, grad, landed, cot, cot_other, weight)


def final_kernel(tab, back_k, back_v, own_k, own_v, grad_k, grad_v, sum_k, sum_v):
    sum_k[1:] = own_k[...].astype(F32)
    sum_v[1:] = own_v[...].astype(F32)

    def add(n, _):
        h = tab[0, T_USED + n]
        sum_k[h] += back_k[0, n].astype(F32)
        sum_v[h] += back_v[0, n].astype(F32)
        return _

    lax.fori_loop(0, 32, add, 0, unroll=4)
    for h in range(HEADS):
        grad_k[:, h * DH : (h + 1) * DH] = sum_k[1 + h].astype(BF16)
        grad_v[:, h * DH : (h + 1) * DH] = sum_v[1 + h].astype(BF16)


def finish(tab, back, own_k, own_v):
    rows = pl.BlockSpec((ROWS, DIM), lambda p, tab: (p, 0))
    own = pl.BlockSpec((HEADS, ROWS, DH), lambda p, tab: (0, p, 0))
    return pl.pallas_call(
        final_kernel,
        out_shape=(
            jax.ShapeDtypeStruct((BLOCK, DIM), BF16),
            jax.ShapeDtypeStruct((BLOCK, DIM), BF16),
        ),
        grid_spec=pltpu.PrefetchScalarGridSpec(
            num_scalar_prefetch=1,
            grid=(HALF,),
            in_specs=[
                pl.BlockSpec((1, 32, ROWS, DH), lambda p, tab: (p, 0, 0, 0)),
                pl.BlockSpec((1, 32, ROWS, DH), lambda p, tab: (p + HALF, 0, 0, 0)),
                own,
                own,
            ],
            out_specs=[rows, rows],
            scratch_shapes=[pltpu.VMEM((HEADS + 1, ROWS, DH), F32)] * 2,
        ),
        compiler_params=pltpu.CompilerParams(vmem_limit_bytes=60 << 20),
        name="finish",
    )(tab, back, back, own_k, own_v)


def per_device(
    query_rows, key_rows, value_rows, cotangent, out_weight, sorted_blocks, window_start
):
    tab = make_tables(sorted_blocks)
    landed, grad, cot_other = fetch(tab, key_rows, value_rows, cotangent, out_weight)
    back, layer, wgrad, grad_q, own_k, own_v = attend(
        tab, window_start, query_rows, key_rows, value_rows, grad, landed,
        cotangent, cot_other, out_weight,
    )
    grad_k, grad_v = finish(tab, back, own_k, own_v)
    return layer, grad_q, grad_k, grad_v, wgrad


def solution(mesh):
    rows = P(("sx", "sy"), None)
    return jax.shard_map(
        per_device,
        mesh=mesh,
        in_specs=(rows, rows, rows, rows, P(), P(), P(None, ("sx", "sy"))),
        out_specs=(rows, rows, rows, rows, rows),
        check_vma=False,
    )
```

```python
import math

import jax
import jax.numpy as jnp
from jax import lax
from jax.experimental import pallas as pl
from jax.experimental.pallas import tpu as pltpu
from jax.sharding import PartitionSpec as P

HEADS = 16
DH = 128
BLOCK = 256
DIM = 2048
PARTS = 8
HALF = PARTS // 2
ROWS = BLOCK // HALF
AHEAD = 2
UNROLL = 4
TWIN = 4
GRAD = 4
JOIN = 2
PAIR = 4
EARLY = 4
TILES = 8
LATE = 7
WHEN = ((7, 9), (6, 7), (6, 7))
SCALE = 1.0 / math.sqrt(DH)
MESH = pl.DeviceIdType.MESH
STREAMS = ((0, 1024, "yzx"), (1024, 512, "xyz"), (1536, 512, "zxy"))
VMEM = pl.BlockSpec(memory_space=pltpu.VMEM)
SMEM = pl.BlockSpec(memory_space=pltpu.SMEM)
ANY = pl.BlockSpec(memory_space=pl.ANY)
NT = (((1,), (1,)), ((), ()))
TN = (((0,), (0,)), ((), ()))
F32 = jnp.float32
BF16 = jnp.bfloat16
T_OUT, T_X, T_BACK, T_Y, T_SLOT, T_HEAD, T_USED = 0, 32, 64, 96, 128, 160, 192


def here():
    outer = lax.axis_index("sx")
    inner = lax.axis_index("sy")
    return (outer // 4) * 2 + inner // 8, outer % 4, (inner // 2) % 4, inner % 2


def place(x, y, z, k):
    return {"sx": (x // 2) * 4 + y, "sy": (x % 2) * 8 + z * 2 + k}


def step_x(pos, d):
    return place((pos[0] + d) % 4, pos[1], pos[2], pos[3])


def step_y(pos, d):
    return place(pos[0], (pos[1] + d) % 4, pos[2], pos[3])


def step_z(pos, dz, dk):
    return place(pos[0], pos[1], (pos[2] + dz) % 4, (pos[3] + dk) % 2)


def greet(pos):
    barrier = pltpu.get_barrier_semaphore()
    peers = [step_x(pos, d) for d in (1, 2, 3)] + [step_y(pos, d) for d in (1, 2, 3)]
    peers += [step_z(pos, j // 2, j % 2) for j in range(1, 8)]
    for peer in peers:
        pl.semaphore_signal(barrier, inc=1, device_id=peer, device_id_type=MESH)
    pl.semaphore_wait(barrier, len(peers))


def send(src, dst, send_sem, recv_sem, peer):
    pltpu.make_async_remote_copy(
        src_ref=src,
        dst_ref=dst,
        send_sem=send_sem,
        recv_sem=recv_sem,
        device_id=peer,
        device_id_type=MESH,
    ).start()


def settle(ref, sem):
    pltpu.make_async_copy(ref, ref, sem).wait()


def table_kernel(src_ref, out_ref):
    x, y, z, k = here()
    device = lax.axis_index("sx") * 16 + lax.axis_index("sy")
    src = src_ref[...]
    head = lax.broadcasted_iota(jnp.int32, src.shape, 0)
    target = lax.broadcasted_iota(jnp.int32, src.shape, 1)
    outer = src >> 4
    nth = jnp.zeros_like(src)
    for h in range(HEADS):
        nth += jnp.where((outer[h : h + 1] == outer) & (head > h), 1, 0)
    rank = jnp.zeros_like(src)
    for d in range(8):
        turned = pltpu.roll(src, 16 * d, axis=1) if d else src
        for h in range(HEADS):
            first = head > h
            if d:
                first = first | ((head == h) & (target >= 16 * d))
            rank += jnp.where((turned[h : h + 1] == src) & first, 1, 0)
    tx = (target >> 6) * 2 + ((target >> 3) & 1)
    ty, tz, tk = (target >> 4) & 3, (target >> 1) & 3, target & 1
    sx = (src >> 6) * 2 + ((src >> 3) & 1)
    sy, sz, sk = (src >> 4) & 3, (src >> 1) & 3, src & 1
    column = (tz == z) & (tk == k)
    to_slot = (tx & 1) * 2 + rank
    out_slot = (((tz - z) & 3) * 2 + (tk ^ k)) * 4 + to_slot
    in_slot = (((z - sz) & 3) * 2 + (k ^ sk)) * 4 + to_slot
    x_slot = ((tx - x) & 3) * 8 + ((ty - y) & 3) * 2 + nth
    passing = column & ((src >> 3) == (device >> 3))
    y_slot = ((ty - y) & 3) * 4 + (sx >> 1) * 2 + nth
    y_from = ((x - sx) & 3) * 8 + ((ty - y) & 3) * 2 + nth
    handing = column & (tx == x) & (sy == y)
    mine = target == device
    my_slot = ((y - sy) & 3) * 4 + (sx >> 1) * 2 + nth
    entries = lax.broadcasted_iota(jnp.int32, (32, 128), 0)
    sums = []
    for chosen, spot, value in (
        (src == device, out_slot, head),
        (passing, x_slot, in_slot),
        (passing, in_slot, x_slot),
        (handing, y_slot, y_from),
        (mine, head, my_slot),
        (mine, my_slot, head),
        (src == device, out_slot, head + 1),
    ):
        spot = jnp.where(chosen, spot, -1)
        total = jnp.zeros((32, 128), jnp.int32)
        for h in range(HEADS):
            total += jnp.where(spot[h : h + 1] == entries, value[h : h + 1], 0)
        sums.append(total.astype(F32))
    sums.append(jnp.zeros((32, 128), F32))
    rows = lax.dot_general(
        jnp.ones((8, 128), F32), jnp.concatenate(sums, axis=0), NT, preferred_element_type=F32
    )
    out_ref[...] = rows.astype(jnp.int32)


def make_tables(sorted_blocks):
    return pl.pallas_call(
        table_kernel,
        out_shape=jax.ShapeDtypeStruct((8, 256), jnp.int32),
        in_specs=[VMEM],
        out_specs=VMEM,
    )(sorted_blocks)


def fetch_kernel(
    tab, key, value, cot, weight, landed, grad_out, cot_other, *scratch
):
    zr, xr, scratch = scratch[:PARTS], scratch[PARTS : 2 * PARTS], scratch[2 * PARTS :]
    wbuf, grad, kv, zs, xs, ys, zss, zrs, xss, xrs, yss, yrs, ysl, cs, cr, wsem, gsem = scratch
    store = pltpu.make_async_copy(grad, grad_out, gsem)
    pos = here()
    load_w = pltpu.make_async_copy(weight, wbuf, wsem)
    load_w.start()

    def gather_z(p):
        ref = key if p < HALF else value
        rows = pl.ds((p % HALF) * ROWS, ROWS)

        for h in range(HEADS):
            kv[p, h] = ref[rows, h * DH : (h + 1) * DH]

        def piece(n):
            return kv[p, tab[0, T_OUT + n]]

        def own(n, _):
            zr[p][n] = piece(n)
            return _

        def other(n, _):
            zs[p, n - 4] = piece(n)
            return _

        lax.fori_loop(0, 4, own, 0, unroll=4)
        lax.fori_loop(4, 32, other, 0, unroll=UNROLL)

    def send_z(p):
        for j in range(1, 8):
            send(
                zs.at[p, pl.ds((j - 1) * 4, 4)], zr[p].at[pl.ds(j * 4, 4)],
                zss.at[p], zrs.at[p], step_z(pos, j // 2, j % 2),
            )

    def pass_x(p):
        settle(zr[p].at[pl.ds(4, 28)], zrs.at[p])

        def own(n, _):
            xr[p][n] = zr[p][tab[0, T_X + n]]
            return _

        def other(n, _):
            xs[p, n - 8] = zr[p][tab[0, T_X + n]]
            return _

        lax.fori_loop(8, 32, other, 0, unroll=UNROLL)
        for d in range(1, 4):
            send(
                xs.at[p, pl.ds((d - 1) * 8, 8)], xr[p].at[pl.ds(d * 8, 8)],
                xss.at[p], xrs.at[p], step_x(pos, d),
            )
        lax.fori_loop(0, 8, own, 0, unroll=UNROLL)

    def pass_y(p):
        settle(xr[p].at[pl.ds(8, 24)], xrs.at[p])

        def each(n, _):
            ys[p, n] = xr[p][tab[0, T_Y + n]]
            return _

        lax.fori_loop(0, 16, each, 0, unroll=UNROLL)
        for d in range(1, 4):
            send(
                ys.at[p, pl.ds(d * 4, 4)], landed.at[p, pl.ds(d * 4, 4)],
                yss.at[p], yrs.at[p], step_y(pos, d),
            )
        pltpu.make_async_copy(
            ys.at[p, pl.ds(0, 4)], landed.at[p, pl.ds(0, 4)], ysl.at[p]
        ).start()

    def grad_tile(c):
        cols = pl.ds(c * 256, 256)
        grad[:, cols] = lax.dot_general(
            cot[...], wbuf[cols, :], NT, preferred_element_type=F32
        ).astype(BF16)

    gather_z(0)
    greet(pos)
    send_z(0)
    for p in range(1, AHEAD):
        gather_z(p)
        send_z(p)
    send(cot, cot_other, cs, cr, step_z(pos, 0, 1))
    for p in range(PARTS):
        if p + AHEAD < PARTS:
            gather_z(p + AHEAD)
            send_z(p + AHEAD)
        pass_x(p)
        if p >= 1:
            pass_y(p - 1)
        if p == GRAD:
            load_w.wait()
            for c in range(8):
                grad_tile(c)
            store.start()
    pass_y(PARTS - 1)
    for p in range(PARTS):
        settle(landed.at[p, pl.ds(4, 12)], yrs.at[p])
        settle(landed.at[p, pl.ds(0, 4)], ysl.at[p])
        settle(zs.at[p], zss.at[p])
        settle(xs.at[p], xss.at[p])
        settle(ys.at[p, pl.ds(4, 12)], yss.at[p])
    settle(cot_other, cr)
    settle(cot, cs)
    store.wait()


def fetch(tab, key, value, cot, weight):
    slot = (ROWS, DH)
    sems = [pltpu.SemaphoreType.DMA((PARTS,))] * 7 + [pltpu.SemaphoreType.DMA] * 4
    return pl.pallas_call(
        fetch_kernel,
        out_shape=(
            jax.ShapeDtypeStruct((PARTS, 16, *slot), BF16),
            jax.ShapeDtypeStruct((BLOCK, DIM), BF16),
            jax.ShapeDtypeStruct((BLOCK, DIM), BF16),
        ),
        in_specs=[SMEM, VMEM, VMEM, VMEM, ANY],
        out_specs=(ANY, ANY, ANY),
        scratch_shapes=[
            *[pltpu.VMEM((32, *slot), BF16)] * (2 * PARTS),
            pltpu.VMEM((DIM, DIM), BF16),
            pltpu.VMEM((BLOCK, DIM), BF16),
            pltpu.VMEM((PARTS, HEADS, *slot), BF16),
            pltpu.VMEM((PARTS, 28, *slot), BF16),
            pltpu.VMEM((PARTS, 24, *slot), BF16),
            pltpu.VMEM((PARTS, 16, *slot), BF16),
            *sems,
        ],
        compiler_params=pltpu.CompilerParams(
            collective_id=0, has_side_effects=True, vmem_limit_bytes=58 << 20
        ),
        name="fetch",
    )(tab, key, value, cot, weight)


AXES = "xyz"


def pick(order, axis, index):
    spot = [slice(None)] * 5
    spot[order.index(axis)] = index
    return tuple(spot[: len(order)])


def attend_kernel(
    tab, start, query, key, value, grad, landed, cot_in, cot_other_in, weight,
    back, layer_out, wgrad, grad_q_out, own_k_out, own_v_out, *scratch
):
    xb, scratch = scratch[:PARTS], scratch[PARTS:]
    (
        q_in, k_in, v_in, g_in, f_in, cot, cot_other, wbuf,
        att, att_t, at_other, pbuf, grad_q, own_k, own_v, layer, terms, ys, yb, zs,
        g0, g1, g2, r10, r11, r12, s10, s11, s12, r20, r21, r22, s20, s21, s22, r30, r31, r32,
        yss, yrs, xss, xrs, zss, zrs, zsl, as_, ar, ins, outs, rs, rr,
    ) = scratch
    pos = here()
    coord = dict(zip(AXES, pos[:3]))
    k = pos[3]
    go = {"x": step_x, "y": step_y, "z": lambda pos, d: step_z(pos, d, 0)}
    g, r1, s1 = (g0, g1, g2), (r10, r11, r12), (s10, s11, s12)
    r2, s2, r3 = (r20, r21, r22), (s20, s21, s22), (r30, r31, r32)
    loads = [
        pltpu.make_async_copy(src, dst, ins.at[n])
        for n, (src, dst) in enumerate(
            (
                (query, q_in), (key, k_in), (landed, f_in), (value, v_in), (grad, g_in),
                (cot_in, cot), (cot_other_in, cot_other), (weight, wbuf),
            )
        )
    ]
    for load in loads[:4]:
        load.start()
    greet(pos)

    def fetched(h, first):
        slot = tab[0, T_SLOT + h]
        return jnp.concatenate([f_in[p, slot] for p in range(first, first + HALF)], axis=0)

    def forward(h, _):
        cols = pl.ds(pl.multiple_of(h * DH, DH), DH)
        qh = q_in[:, cols]
        own = lax.dot_general(qh, k_in[:, cols], NT, preferred_element_type=F32) * SCALE
        spot = lax.broadcasted_iota(jnp.int32, own.shape, 1)
        own = jnp.where(spot >= start[0, h], own, -jnp.inf)
        far = lax.dot_general(qh, fetched(h, 0), NT, preferred_element_type=F32) * SCALE
        top = jnp.max(jnp.maximum(own, far), axis=1, keepdims=True)
        own, far = jnp.exp(own - top), jnp.exp(far - top)
        share = 1.0 / jnp.sum(own + far, axis=1, keepdims=True)
        own, far = own * share, far * share
        pbuf[h, 0] = own
        pbuf[h, 1] = far
        a = jnp.dot(own.astype(BF16), v_in[:, cols], preferred_element_type=F32)
        a += jnp.dot(far.astype(BF16), fetched(h, HALF), preferred_element_type=F32)
        a = a.astype(BF16)
        att[:, cols] = a
        att_t[h] = a.astype(F32).T.astype(BF16).reshape(4, 2, 16, BLOCK)
        return _

    def backward(h, _):
        cols = pl.ds(pl.multiple_of(h * DH, DH), DH)
        gh, qh, probs = g_in[:, cols], q_in[:, cols], pbuf[h, 1]
        delta = jnp.sum(gh.astype(F32) * att[:, cols].astype(F32), axis=1, keepdims=True)
        pg = lax.dot_general(gh, fetched(h, HALF), NT, preferred_element_type=F32)
        ds = (probs * (pg - delta)).astype(BF16)
        kt = lax.dot_general(ds, qh, TN, preferred_element_type=F32) * SCALE
        vt = lax.dot_general(probs.astype(BF16), gh, TN, preferred_element_type=F32)
        pbuf[h, 1] = ds.astype(F32)
        for p in range(HALF):
            rows = slice(p * ROWS, (p + 1) * ROWS)
            terms[p, h] = kt[rows].astype(BF16)
            terms[p + HALF, h] = vt[rows].astype(BF16)
        return _

    def backward_own(h, _):
        cols = pl.ds(pl.multiple_of(h * DH, DH), DH)
        gh, qh, kh, probs = g_in[:, cols], q_in[:, cols], k_in[:, cols], pbuf[h, 0]
        delta = jnp.sum(gh.astype(F32) * att[:, cols].astype(F32), axis=1, keepdims=True)
        pg = lax.dot_general(gh, v_in[:, cols], NT, preferred_element_type=F32)
        ds = (probs * (pg - delta)).astype(BF16)
        gq = jnp.dot(ds, kh, preferred_element_type=F32)
        gq += jnp.dot(pbuf[h, 1].astype(BF16), fetched(h, 0), preferred_element_type=F32)
        grad_q[:, cols] = (gq * SCALE).astype(BF16)
        kt = lax.dot_general(ds, qh, TN, preferred_element_type=F32) * SCALE
        vt = lax.dot_general(probs.astype(BF16), gh, TN, preferred_element_type=F32)
        own_k[h] = kt.astype(BF16)
        own_v[h] = vt.astype(BF16)
        return _

    for load in loads[:4]:
        load.wait()
    for load in loads[4:7]:
        load.start()
    lax.fori_loop(0, HEADS, forward, 0, unroll=PAIR)
    send(att_t.at[:, :, 1 - k], at_other, as_, ar, step_z(pos, 0, 1))
    for load in loads[4:7]:
        load.wait()
    lax.fori_loop(0, EARLY, backward, 0, unroll=TWIN)
    settle(at_other, ar)

    def partial(n):
        first, width, _ = STREAMS[n]

        def tile(m, c):
            cols = pl.ds(pl.multiple_of(first + c * 256, 256), 256)
            mine = att_t[pl.ds(m * 4, 4), :, k].reshape(256, BLOCK)
            theirs = at_other[pl.ds(m * 4, 4)].reshape(256, BLOCK)
            t = jnp.dot(mine, cot[:, cols], preferred_element_type=F32)
            t += jnp.dot(theirs, cot_other[:, cols], preferred_element_type=F32)
            t = t.astype(BF16).reshape(4, 4, 16, 256)
            out = pl.ds(pl.multiple_of(c * 256, 256), 256)
            for i in range(4):
                g[n][(m // 2) * 2 + i % 2, (m % 2) * 2 + i // 2, :, :, out] = t[i]

        def tiles(i, _):
            tile(i % 4, i // 4)
            return _

        lax.fori_loop(0, 4 * (width // 256), tiles, 0, unroll=TILES)

    def send_one(n):
        a = STREAMS[n][2][0]
        for d in range(1, 4):
            send(
                g[n].at[pick(AXES, a, (coord[a] + d) % 4)], r1[n].at[d - 1],
                rs.at[n, 0], rr.at[n, 0], go[a](pos, d),
            )

    loads[7].start()
    for n in (2, 1):
        partial(n)
        send_one(n)
    lax.fori_loop(EARLY, HEADS, backward, 0, unroll=TWIN)

    def return_y(p):
        def own(n, _):
            yb[p, 0, n] = terms[p, tab[0, T_HEAD + n]]
            return _

        def other(n, _):
            ys[p, n - 4] = terms[p, tab[0, T_HEAD + n]]
            return _

        lax.fori_loop(4, 16, other, 0, unroll=4)
        for d in range(1, 4):
            send(
                ys.at[p, pl.ds(d * 4 - 4, 4)], yb.at[p, d], yss.at[p], yrs.at[p],
                step_y(pos, 4 - d),
            )
        lax.fori_loop(0, 4, own, 0, unroll=4)

    def return_x(p):
        settle(yb.at[p, pl.ds(1, 3)], yrs.at[p])
        for d in range(4):
            half = ((pos[0] + 4 - d) % 4) // 2
            src = yb.at[p, :, pl.ds(half * 2, 2)]
            if d:
                send(src, xb[p].at[d], xss.at[p], xrs.at[p], step_x(pos, 4 - d))
            else:
                xb[p][0] = yb[p, :, pl.ds(half * 2, 2)]

    def return_z(p):
        settle(xb[p].at[pl.ds(1, 3)], xrs.at[p])

        def each(n, _):
            e = tab[0, T_BACK + n]
            zs[p, n] = xb[p][e // 8, (e // 2) % 4, e % 2]
            return _

        lax.fori_loop(0, 32, each, 0, unroll=UNROLL)
        for j in range(1, 8):
            send(
                zs.at[p, pl.ds(j * 4, 4)], back.at[p, pl.ds(j * 4, 4)],
                zss.at[p], zrs.at[p], step_z(pos, 4 - j // 2, j % 2),
            )
        pltpu.make_async_copy(
            zs.at[p, pl.ds(0, 4)], back.at[p, pl.ds(0, 4)], zsl.at[p]
        ).start()

    def sum_one(n):
        order = STREAMS[n][2]
        a = order[0]
        rest = [b for b in AXES if b != a]
        settle(r1[n], rr.at[n, 0])
        settle(r1[n], rs.at[n, 0])

        def each(i, _):
            at = (i // 4, i % 4)
            spot = list(at)
            spot.insert(AXES.index(a), coord[a])
            t = g[n][tuple(spot)].astype(F32)
            for d in range(3):
                t += r1[n][(d, *at)].astype(F32)
            s1[n][at] = t.astype(BF16)
            return _

        lax.fori_loop(0, 16, each, 0)
        b = order[1]
        for d in range(1, 4):
            send(
                s1[n].at[pick(rest, b, (coord[b] + d) % 4)], r2[n].at[d - 1],
                rs.at[n, 1], rr.at[n, 1], go[b](pos, d),
            )

    def sum_two(n):
        order = STREAMS[n][2]
        rest = [b for b in AXES if b != order[0]]
        settle(r2[n], rr.at[n, 1])
        settle(r2[n], rs.at[n, 1])
        b, c = order[1], order[2]
        for i in range(4):
            spot = [i]
            spot.insert(rest.index(b), coord[b])
            t = s1[n][tuple(spot)].astype(F32)
            for d in range(3):
                t += r2[n][d, i].astype(F32)
            s2[n][i] = t.astype(BF16)
        for d in range(1, 4):
            send(
                s2[n].at[(coord[c] + d) % 4], r3[n].at[d - 1],
                rs.at[n, 2], rr.at[n, 2], go[c](pos, d),
            )

    def sum_three(n):
        first, width, order = STREAMS[n]
        settle(r3[n], rr.at[n, 2])
        settle(r3[n], rs.at[n, 2])
        t = s2[n][coord[order[2]]].astype(F32)
        for d in range(3):
            t += r3[n][d].astype(F32)
        wgrad[:, pl.ds(first, width)] = t * (1.0 / math.sqrt(BLOCK * 128))

    def layer_tile(c, _):
        cols = pl.ds(pl.multiple_of(c * 256, 256), 256)
        layer[:, cols] = jnp.dot(
            att[...], wbuf[:, cols], preferred_element_type=F32
        ).astype(BF16)
        return _

    stores = [
        pltpu.make_async_copy(src, dst, outs.at[n])
        for n, (src, dst) in enumerate(
            ((grad_q, grad_q_out), (own_k, own_k_out), (own_v, own_v_out), (layer, layer_out))
        )
    ]
    for p in range(PARTS):
        return_y(p)
        if p == LATE:
            partial(0)
    send_one(0)
    each = HEADS // PARTS
    for p in range(PARTS):
        return_x(p)
        if p >= 1:
            return_z(p - 1)
        if p == 1:
            loads[7].wait()
            lax.fori_loop(0, 8, layer_tile, 0)
            stores[3].start()
        lax.fori_loop(p * each, (p + 1) * each, backward_own, 0, unroll=each)
        for level, step in enumerate((sum_one, sum_two)):
            for n in range(3):
                if WHEN[n][level] == p:
                    step(n)
    for store in stores[:3]:
        store.start()
    return_z(PARTS - 1)
    for n in (1, 2):
        sum_three(n)
    sum_two(0)
    sum_three(0)
    for p in range(PARTS):
        settle(back.at[p, pl.ds(4, 28)], zrs.at[p])
        settle(back.at[p, pl.ds(0, 4)], zsl.at[p])
        settle(zs.at[p, pl.ds(4, 28)], zss.at[p])
        settle(xb[p].at[pl.ds(1, 3)], xss.at[p])
        settle(ys.at[p], yss.at[p])
    settle(at_other, as_)
    for store in stores:
        store.wait()


def attend(tab, start, query, key, value, grad, landed, cot, cot_other, weight):
    slot = (ROWS, DH)
    tokens = (BLOCK, DIM)
    widths = [w for _, w, _ in STREAMS]
    per_stream = [
        [pltpu.VMEM((*lead, 16, w), BF16) for w in widths]
        for lead in ((4, 4, 4), (3, 4, 4), (4, 4), (3, 4), (4,), (3,))
    ]
    return pl.pallas_call(
        attend_kernel,
        out_shape=(
            jax.ShapeDtypeStruct((PARTS, 32, *slot), BF16),
            jax.ShapeDtypeStruct(tokens, BF16),
            jax.ShapeDtypeStruct((16, DIM), F32),
            jax.ShapeDtypeStruct(tokens, BF16),
            jax.ShapeDtypeStruct((HEADS, BLOCK, DH), BF16),
            jax.ShapeDtypeStruct((HEADS, BLOCK, DH), BF16),
        ),
        in_specs=[SMEM, SMEM, *[ANY] * 8],
        out_specs=(ANY, ANY, VMEM, ANY, ANY, ANY),
        scratch_shapes=[
            *[pltpu.VMEM((4, 4, 2, *slot), BF16)] * PARTS,
            *[pltpu.VMEM(tokens, BF16)] * 4,
            pltpu.VMEM((PARTS, 16, *slot), BF16),
            *[pltpu.VMEM(tokens, BF16)] * 2,
            pltpu.VMEM((DIM, DIM), BF16),
            pltpu.VMEM(tokens, BF16),
            pltpu.VMEM((HEADS, 4, 2, 16, BLOCK), BF16),
            pltpu.VMEM((HEADS, 4, 16, BLOCK), BF16),
            pltpu.VMEM((HEADS, 2, BLOCK, BLOCK), F32),
            pltpu.VMEM(tokens, BF16),
            pltpu.VMEM((HEADS, BLOCK, DH), BF16),
            pltpu.VMEM((HEADS, BLOCK, DH), BF16),
            pltpu.VMEM(tokens, BF16),
            pltpu.VMEM((PARTS, 16, *slot), BF16),
            pltpu.VMEM((PARTS, 12, *slot), BF16),
            pltpu.VMEM((PARTS, 4, 4, *slot), BF16),
            pltpu.VMEM((PARTS, 32, *slot), BF16),
            *[buf for level in per_stream for buf in level],
            *[pltpu.SemaphoreType.DMA((PARTS,))] * 7,
            *[pltpu.SemaphoreType.DMA] * 2,
            pltpu.SemaphoreType.DMA((8,)),
            pltpu.SemaphoreType.DMA((4,)),
            pltpu.SemaphoreType.DMA((3, 3)),
            pltpu.SemaphoreType.DMA((3, 3)),
        ],
        compiler_params=pltpu.CompilerParams(
            collective_id=1, has_side_effects=True, vmem_limit_bytes=62 << 20
        ),
        name="attend",
    )(tab, start, query, key, value, grad, landed, cot, cot_other, weight)


def final_kernel(
    tab, back_k, back_v, own_k, own_v, layer, grad_q, wgrad,
    grad_k, grad_v, layer_out, grad_q_out, wgrad_out, *sums
):
    layer_out[...] = layer[...]
    grad_q_out[...] = grad_q[...]
    wgrad_out[...] = wgrad[...]

    parts = [(back, own, i) for i in range(JOIN) for back, own in ((back_k, own_k), (back_v, own_v))]
    for total, (_, own, i) in zip(sums, parts):
        total[1:] = own[:, i * ROWS : (i + 1) * ROWS].astype(F32)

    def add(n, carry):
        h = tab[0, T_USED + n]
        for total, (back, _, i) in zip(sums, parts):
            total[h] += back[i, n].astype(F32)
        return carry

    lax.fori_loop(0, 32, add, 0, unroll=4)
    for h in range(HEADS):
        for total, (back, _, i) in zip(sums, parts):
            out = grad_k if back is back_k else grad_v
            out[i * ROWS : (i + 1) * ROWS, h * DH : (h + 1) * DH] = total[1 + h].astype(BF16)


def finish(tab, back, own_k, own_v, layer, grad_q, wgrad):
    steps = HALF // JOIN
    rows = pl.BlockSpec((ROWS * JOIN, DIM), lambda p, tab: (p, 0))
    own = pl.BlockSpec((HEADS, ROWS * JOIN, DH), lambda p, tab: (0, p, 0))
    whole = pl.BlockSpec((16, DIM), lambda p, tab: (0, 0))
    tokens = jax.ShapeDtypeStruct((BLOCK, DIM), BF16)
    return pl.pallas_call(
        final_kernel,
        out_shape=(tokens, tokens, tokens, tokens, jax.ShapeDtypeStruct((16, DIM), F32)),
        grid_spec=pltpu.PrefetchScalarGridSpec(
            num_scalar_prefetch=1,
            grid=(steps,),
            in_specs=[
                pl.BlockSpec((JOIN, 32, ROWS, DH), lambda p, tab: (p, 0, 0, 0)),
                pl.BlockSpec((JOIN, 32, ROWS, DH), lambda p, tab: (p + steps, 0, 0, 0)),
                own, own, rows, rows, whole,
            ],
            out_specs=[rows, rows, rows, rows, whole],
            scratch_shapes=[
                *[pltpu.VMEM((HEADS + 1, ROWS, DH), F32)] * (2 * JOIN),
            ],
        ),
        compiler_params=pltpu.CompilerParams(vmem_limit_bytes=60 << 20),
        name="finish",
    )(tab, back, back, own_k, own_v, layer, grad_q, wgrad)


def per_device(
    query_rows, key_rows, value_rows, cotangent, out_weight, sorted_blocks, window_start
):
    tab = make_tables(sorted_blocks)
    landed, grad, cot_other = fetch(tab, key_rows, value_rows, cotangent, out_weight)
    back, layer, wgrad, grad_q, own_k, own_v = attend(
        tab, window_start.reshape(1, HEADS), query_rows, key_rows, value_rows, grad, landed,
        cotangent, cot_other, out_weight,
    )
    grad_k, grad_v, layer, grad_q, wgrad = finish(
        tab, back, own_k, own_v, layer, grad_q, wgrad
    )
    return layer, grad_q, grad_k, grad_v, wgrad


def solution(mesh):
    rows = P(("sx", "sy"), None)
    return jax.shard_map(
        per_device,
        mesh=mesh,
        in_specs=(rows, rows, rows, rows, P(), P(), P(None, ("sx", "sy"))),
        out_specs=(rows, rows, rows, rows, rows),
        check_vma=False,
    )
```

```python
import math

import jax
import jax.numpy as jnp
from jax import lax
from jax.experimental import pallas as pl
from jax.experimental.pallas import tpu as pltpu
from jax.sharding import PartitionSpec as P

HEADS = 16
DH = 128
BLOCK = 256
DIM = 2048
PARTS = 8
HALF = PARTS // 2
ROWS = BLOCK // HALF
AHEAD = 2
UNROLL = 4
TWIN = 4
GRAD = 4
JOIN = 2
PAIR = 4
EARLY = 4
TILES = 8
LATE = 0
WHEN = ((7, 9), (6, 7), (6, 7))
SCALE = 1.0 / math.sqrt(DH)
MESH = pl.DeviceIdType.MESH
STREAMS = ((0, 1024, "yzx"), (1024, 512, "xyz"), (1536, 512, "zxy"))
VMEM = pl.BlockSpec(memory_space=pltpu.VMEM)
SMEM = pl.BlockSpec(memory_space=pltpu.SMEM)
ANY = pl.BlockSpec(memory_space=pl.ANY)
NT = (((1,), (1,)), ((), ()))
TN = (((0,), (0,)), ((), ()))
F32 = jnp.float32
BF16 = jnp.bfloat16
T_OUT, T_X, T_BACK, T_Y, T_SLOT, T_HEAD, T_USED = 0, 32, 64, 96, 128, 160, 192


def here():
    outer = lax.axis_index("sx")
    inner = lax.axis_index("sy")
    return (outer // 4) * 2 + inner // 8, outer % 4, (inner // 2) % 4, inner % 2


def place(x, y, z, k):
    return {"sx": (x // 2) * 4 + y, "sy": (x % 2) * 8 + z * 2 + k}


def step_x(pos, d):
    return place((pos[0] + d) % 4, pos[1], pos[2], pos[3])


def step_y(pos, d):
    return place(pos[0], (pos[1] + d) % 4, pos[2], pos[3])


def step_z(pos, dz, dk):
    return place(pos[0], pos[1], (pos[2] + dz) % 4, (pos[3] + dk) % 2)


def greet(pos):
    barrier = pltpu.get_barrier_semaphore()
    peers = [step_x(pos, d) for d in (1, 2, 3)] + [step_y(pos, d) for d in (1, 2, 3)]
    peers += [step_z(pos, j // 2, j % 2) for j in range(1, 8)]
    for peer in peers:
        pl.semaphore_signal(barrier, inc=1, device_id=peer, device_id_type=MESH)
    pl.semaphore_wait(barrier, len(peers))


def send(src, dst, send_sem, recv_sem, peer):
    pltpu.make_async_remote_copy(
        src_ref=src,
        dst_ref=dst,
        send_sem=send_sem,
        recv_sem=recv_sem,
        device_id=peer,
        device_id_type=MESH,
    ).start()


def settle(ref, sem):
    pltpu.make_async_copy(ref, ref, sem).wait()


def table_kernel(src_ref, out_ref):
    x, y, z, k = here()
    device = lax.axis_index("sx") * 16 + lax.axis_index("sy")
    src = src_ref[...]
    head = lax.broadcasted_iota(jnp.int32, src.shape, 0)
    target = lax.broadcasted_iota(jnp.int32, src.shape, 1)
    outer = src >> 4
    nth = jnp.zeros_like(src)
    for h in range(HEADS):
        nth += jnp.where((outer[h : h + 1] == outer) & (head > h), 1, 0)
    rank = jnp.zeros_like(src)
    for d in range(8):
        turned = pltpu.roll(src, 16 * d, axis=1) if d else src
        for h in range(HEADS):
            first = head > h
            if d:
                first = first | ((head == h) & (target >= 16 * d))
            rank += jnp.where((turned[h : h + 1] == src) & first, 1, 0)
    tx = (target >> 6) * 2 + ((target >> 3) & 1)
    ty, tz, tk = (target >> 4) & 3, (target >> 1) & 3, target & 1
    sx = (src >> 6) * 2 + ((src >> 3) & 1)
    sy, sz, sk = (src >> 4) & 3, (src >> 1) & 3, src & 1
    column = (tz == z) & (tk == k)
    to_slot = (tx & 1) * 2 + rank
    out_slot = (((tz - z) & 3) * 2 + (tk ^ k)) * 4 + to_slot
    in_slot = (((z - sz) & 3) * 2 + (k ^ sk)) * 4 + to_slot
    x_slot = ((tx - x) & 3) * 8 + ((ty - y) & 3) * 2 + nth
    passing = column & ((src >> 3) == (device >> 3))
    y_slot = ((ty - y) & 3) * 4 + (sx >> 1) * 2 + nth
    y_from = ((x - sx) & 3) * 8 + ((ty - y) & 3) * 2 + nth
    handing = column & (tx == x) & (sy == y)
    mine = target == device
    my_slot = ((y - sy) & 3) * 4 + (sx >> 1) * 2 + nth
    entries = lax.broadcasted_iota(jnp.int32, (32, 128), 0)
    sums = []
    for chosen, spot, value in (
        (src == device, out_slot, head),
        (passing, x_slot, in_slot),
        (passing, in_slot, x_slot),
        (handing, y_slot, y_from),
        (mine, head, my_slot),
        (mine, my_slot, head),
        (src == device, out_slot, head + 1),
    ):
        spot = jnp.where(chosen, spot, -1)
        total = jnp.zeros((32, 128), jnp.int32)
        for h in range(HEADS):
            total += jnp.where(spot[h : h + 1] == entries, value[h : h + 1], 0)
        sums.append(total.astype(F32))
    sums.append(jnp.zeros((32, 128), F32))
    rows = lax.dot_general(
        jnp.ones((8, 128), F32), jnp.concatenate(sums, axis=0), NT, preferred_element_type=F32
    )
    out_ref[...] = rows.astype(jnp.int32)


def make_tables(sorted_blocks):
    return pl.pallas_call(
        table_kernel,
        out_shape=jax.ShapeDtypeStruct((8, 256), jnp.int32),
        in_specs=[VMEM],
        out_specs=VMEM,
    )(sorted_blocks)


def fetch_kernel(
    tab, key, value, cot, weight, landed, grad_out, cot_other, *scratch
):
    zr, xr, scratch = scratch[:PARTS], scratch[PARTS : 2 * PARTS], scratch[2 * PARTS :]
    wbuf, grad, kv, zs, xs, ys, zss, zrs, xss, xrs, yss, yrs, ysl, cs, cr, wsem, gsem = scratch
    store = pltpu.make_async_copy(grad, grad_out, gsem)
    pos = here()
    load_w = pltpu.make_async_copy(weight, wbuf, wsem)
    load_w.start()

    def gather_z(p):
        ref = key if p < HALF else value
        rows = pl.ds((p % HALF) * ROWS, ROWS)

        for h in range(HEADS):
            kv[p, h] = ref[rows, h * DH : (h + 1) * DH]

        def piece(n):
            return kv[p, tab[0, T_OUT + n]]

        def own(n, _):
            zr[p][n] = piece(n)
            return _

        def other(n, _):
            zs[p, n - 4] = piece(n)
            return _

        lax.fori_loop(0, 4, own, 0, unroll=4)
        lax.fori_loop(4, 32, other, 0, unroll=UNROLL)

    def send_z(p):
        for j in range(1, 8):
            send(
                zs.at[p, pl.ds((j - 1) * 4, 4)], zr[p].at[pl.ds(j * 4, 4)],
                zss.at[p], zrs.at[p], step_z(pos, j // 2, j % 2),
            )

    def pass_x(p):
        settle(zr[p].at[pl.ds(4, 28)], zrs.at[p])

        def own(n, _):
            xr[p][n] = zr[p][tab[0, T_X + n]]
            return _

        def other(n, _):
            xs[p, n - 8] = zr[p][tab[0, T_X + n]]
            return _

        lax.fori_loop(8, 32, other, 0, unroll=UNROLL)
        for d in range(1, 4):
            send(
                xs.at[p, pl.ds((d - 1) * 8, 8)], xr[p].at[pl.ds(d * 8, 8)],
                xss.at[p], xrs.at[p], step_x(pos, d),
            )
        lax.fori_loop(0, 8, own, 0, unroll=UNROLL)

    def pass_y(p):
        settle(xr[p].at[pl.ds(8, 24)], xrs.at[p])

        def each(n, _):
            ys[p, n] = xr[p][tab[0, T_Y + n]]
            return _

        lax.fori_loop(0, 16, each, 0, unroll=UNROLL)
        for d in range(1, 4):
            send(
                ys.at[p, pl.ds(d * 4, 4)], landed.at[p, pl.ds(d * 4, 4)],
                yss.at[p], yrs.at[p], step_y(pos, d),
            )
        pltpu.make_async_copy(
            ys.at[p, pl.ds(0, 4)], landed.at[p, pl.ds(0, 4)], ysl.at[p]
        ).start()

    def grad_tile(c):
        cols = pl.ds(c * 256, 256)
        grad[:, cols] = lax.dot_general(
            cot[...], wbuf[cols, :], NT, preferred_element_type=F32
        ).astype(BF16)

    gather_z(0)
    greet(pos)
    send_z(0)
    for p in range(1, AHEAD):
        gather_z(p)
        send_z(p)
    send(cot, cot_other, cs, cr, step_z(pos, 0, 1))
    for p in range(PARTS):
        if p + AHEAD < PARTS:
            gather_z(p + AHEAD)
            send_z(p + AHEAD)
        pass_x(p)
        if p >= 1:
            pass_y(p - 1)
        if p == GRAD:
            load_w.wait()
            for c in range(8):
                grad_tile(c)
            store.start()
    pass_y(PARTS - 1)
    for p in range(PARTS):
        settle(landed.at[p, pl.ds(4, 12)], yrs.at[p])
        settle(landed.at[p, pl.ds(0, 4)], ysl.at[p])
        settle(zs.at[p], zss.at[p])
        settle(xs.at[p], xss.at[p])
        settle(ys.at[p, pl.ds(4, 12)], yss.at[p])
    settle(cot_other, cr)
    settle(cot, cs)
    store.wait()


def fetch(tab, key, value, cot, weight):
    slot = (ROWS, DH)
    sems = [pltpu.SemaphoreType.DMA((PARTS,))] * 7 + [pltpu.SemaphoreType.DMA] * 4
    return pl.pallas_call(
        fetch_kernel,
        out_shape=(
            jax.ShapeDtypeStruct((PARTS, 16, *slot), BF16),
            jax.ShapeDtypeStruct((BLOCK, DIM), BF16),
            jax.ShapeDtypeStruct((BLOCK, DIM), BF16),
        ),
        in_specs=[SMEM, VMEM, VMEM, VMEM, ANY],
        out_specs=(ANY, ANY, ANY),
        scratch_shapes=[
            *[pltpu.VMEM((32, *slot), BF16)] * (2 * PARTS),
            pltpu.VMEM((DIM, DIM), BF16),
            pltpu.VMEM((BLOCK, DIM), BF16),
            pltpu.VMEM((PARTS, HEADS, *slot), BF16),
            pltpu.VMEM((PARTS, 28, *slot), BF16),
            pltpu.VMEM((PARTS, 24, *slot), BF16),
            pltpu.VMEM((PARTS, 16, *slot), BF16),
            *sems,
        ],
        compiler_params=pltpu.CompilerParams(
            collective_id=0, has_side_effects=True, vmem_limit_bytes=58 << 20
        ),
        name="fetch",
    )(tab, key, value, cot, weight)


AXES = "xyz"


def pick(order, axis, index):
    spot = [slice(None)] * 5
    spot[order.index(axis)] = index
    return tuple(spot[: len(order)])


def attend_kernel(
    tab, start, query, key, value, grad, landed, cot_in, cot_other_in, weight,
    back, layer_out, wgrad, grad_q_out, own_k_out, own_v_out, *scratch
):
    xb, scratch = scratch[:PARTS], scratch[PARTS:]
    (
        q_in, k_in, v_in, g_in, f_in, cot, cot_other, wbuf,
        att, att_t, at_other, pbuf, grad_q, own_k, own_v, layer, terms, ys, yb, zs,
        g0, g1, g2, r10, r11, r12, s10, s11, s12, r20, r21, r22, s20, s21, s22, r30, r31, r32,
        yss, yrs, xss, xrs, zss, zrs, zsl, as_, ar, ins, outs, rs, rr,
    ) = scratch
    pos = here()
    coord = dict(zip(AXES, pos[:3]))
    k = pos[3]
    go = {"x": step_x, "y": step_y, "z": lambda pos, d: step_z(pos, d, 0)}
    g, r1, s1 = (g0, g1, g2), (r10, r11, r12), (s10, s11, s12)
    r2, s2, r3 = (r20, r21, r22), (s20, s21, s22), (r30, r31, r32)
    loads = [
        pltpu.make_async_copy(src, dst, ins.at[n])
        for n, (src, dst) in enumerate(
            (
                (query, q_in), (key, k_in), (landed, f_in), (value, v_in), (grad, g_in),
                (cot_in, cot), (cot_other_in, cot_other), (weight, wbuf),
            )
        )
    ]
    for load in loads[:4]:
        load.start()
    greet(pos)

    def fetched(h, first):
        slot = tab[0, T_SLOT + h]
        return jnp.concatenate([f_in[p, slot] for p in range(first, first + HALF)], axis=0)

    def forward(h, _):
        cols = pl.ds(pl.multiple_of(h * DH, DH), DH)
        qh = q_in[:, cols]
        own = lax.dot_general(qh, k_in[:, cols], NT, preferred_element_type=F32) * SCALE
        spot = lax.broadcasted_iota(jnp.int32, own.shape, 1)
        own = jnp.where(spot >= start[0, h], own, -jnp.inf)
        far = lax.dot_general(qh, fetched(h, 0), NT, preferred_element_type=F32) * SCALE
        top = jnp.max(jnp.maximum(own, far), axis=1, keepdims=True)
        own, far = jnp.exp(own - top), jnp.exp(far - top)
        share = 1.0 / jnp.sum(own + far, axis=1, keepdims=True)
        own, far = own * share, far * share
        pbuf[h, 0] = own
        pbuf[h, 1] = far
        a = jnp.dot(own.astype(BF16), v_in[:, cols], preferred_element_type=F32)
        a += jnp.dot(far.astype(BF16), fetched(h, HALF), preferred_element_type=F32)
        a = a.astype(BF16)
        att[:, cols] = a
        att_t[h] = a.astype(F32).T.astype(BF16).reshape(4, 2, 16, BLOCK)
        return _

    def backward(h, _):
        cols = pl.ds(pl.multiple_of(h * DH, DH), DH)
        gh, qh, probs = g_in[:, cols], q_in[:, cols], pbuf[h, 1]
        delta = jnp.sum(gh.astype(F32) * att[:, cols].astype(F32), axis=1, keepdims=True)
        pg = lax.dot_general(gh, fetched(h, HALF), NT, preferred_element_type=F32)
        ds = (probs * (pg - delta)).astype(BF16)
        kt = lax.dot_general(ds, qh, TN, preferred_element_type=F32) * SCALE
        vt = lax.dot_general(probs.astype(BF16), gh, TN, preferred_element_type=F32)
        pbuf[h, 1] = ds.astype(F32)
        for p in range(HALF):
            rows = slice(p * ROWS, (p + 1) * ROWS)
            terms[p, h] = kt[rows].astype(BF16)
            terms[p + HALF, h] = vt[rows].astype(BF16)
        return _

    def backward_own(h, _):
        cols = pl.ds(pl.multiple_of(h * DH, DH), DH)
        gh, qh, kh, probs = g_in[:, cols], q_in[:, cols], k_in[:, cols], pbuf[h, 0]
        delta = jnp.sum(gh.astype(F32) * att[:, cols].astype(F32), axis=1, keepdims=True)
        pg = lax.dot_general(gh, v_in[:, cols], NT, preferred_element_type=F32)
        ds = (probs * (pg - delta)).astype(BF16)
        gq = jnp.dot(ds, kh, preferred_element_type=F32)
        gq += jnp.dot(pbuf[h, 1].astype(BF16), fetched(h, 0), preferred_element_type=F32)
        grad_q[:, cols] = (gq * SCALE).astype(BF16)
        kt = lax.dot_general(ds, qh, TN, preferred_element_type=F32) * SCALE
        vt = lax.dot_general(probs.astype(BF16), gh, TN, preferred_element_type=F32)
        own_k[h] = kt.astype(BF16)
        own_v[h] = vt.astype(BF16)
        return _

    for load in loads[:4]:
        load.wait()
    for load in loads[4:7]:
        load.start()
    lax.fori_loop(0, HEADS, forward, 0, unroll=PAIR)
    send(att_t.at[:, :, 1 - k], at_other, as_, ar, step_z(pos, 0, 1))
    for load in loads[4:7]:
        load.wait()
    lax.fori_loop(0, EARLY, backward, 0, unroll=TWIN)
    settle(at_other, ar)

    def partial(n):
        first, width, _ = STREAMS[n]

        def tile(m, c):
            cols = pl.ds(pl.multiple_of(first + c * 256, 256), 256)
            mine = att_t[pl.ds(m * 4, 4), :, k].reshape(256, BLOCK)
            theirs = at_other[pl.ds(m * 4, 4)].reshape(256, BLOCK)
            t = jnp.dot(mine, cot[:, cols], preferred_element_type=F32)
            t += jnp.dot(theirs, cot_other[:, cols], preferred_element_type=F32)
            t = t.astype(BF16).reshape(4, 4, 16, 256)
            out = pl.ds(pl.multiple_of(c * 256, 256), 256)
            for i in range(4):
                g[n][(m // 2) * 2 + i % 2, (m % 2) * 2 + i // 2, :, :, out] = t[i]

        def tiles(i, _):
            tile(i % 4, i // 4)
            return _

        lax.fori_loop(0, 4 * (width // 256), tiles, 0, unroll=TILES)

    def send_one(n):
        a = STREAMS[n][2][0]
        for d in range(1, 4):
            send(
                g[n].at[pick(AXES, a, (coord[a] + d) % 4)], r1[n].at[d - 1],
                rs.at[n, 0], rr.at[n, 0], go[a](pos, d),
            )

    loads[7].start()
    for n in (2, 1):
        partial(n)
        send_one(n)
    lax.fori_loop(EARLY, HEADS, backward, 0, unroll=TWIN)

    def return_y(p):
        def own(n, _):
            yb[p, 0, n] = terms[p, tab[0, T_HEAD + n]]
            return _

        def other(n, _):
            ys[p, n - 4] = terms[p, tab[0, T_HEAD + n]]
            return _

        lax.fori_loop(4, 16, other, 0, unroll=4)
        for d in range(1, 4):
            send(
                ys.at[p, pl.ds(d * 4 - 4, 4)], yb.at[p, d], yss.at[p], yrs.at[p],
                step_y(pos, 4 - d),
            )
        lax.fori_loop(0, 4, own, 0, unroll=4)

    def return_x(p):
        settle(yb.at[p, pl.ds(1, 3)], yrs.at[p])
        for d in range(4):
            half = ((pos[0] + 4 - d) % 4) // 2
            src = yb.at[p, :, pl.ds(half * 2, 2)]
            if d:
                send(src, xb[p].at[d], xss.at[p], xrs.at[p], step_x(pos, 4 - d))
            else:
                xb[p][0] = yb[p, :, pl.ds(half * 2, 2)]

    def return_z(p):
        settle(xb[p].at[pl.ds(1, 3)], xrs.at[p])

        def each(n, _):
            e = tab[0, T_BACK + n]
            zs[p, n] = xb[p][e // 8, (e // 2) % 4, e % 2]
            return _

        lax.fori_loop(0, 32, each, 0, unroll=UNROLL)
        for j in range(1, 8):
            send(
                zs.at[p, pl.ds(j * 4, 4)], back.at[p, pl.ds(j * 4, 4)],
                zss.at[p], zrs.at[p], step_z(pos, 4 - j // 2, j % 2),
            )
        pltpu.make_async_copy(
            zs.at[p, pl.ds(0, 4)], back.at[p, pl.ds(0, 4)], zsl.at[p]
        ).start()

    def sum_one(n):
        order = STREAMS[n][2]
        a = order[0]
        rest = [b for b in AXES if b != a]
        settle(r1[n], rr.at[n, 0])
        settle(r1[n], rs.at[n, 0])

        def each(i, _):
            at = (i // 4, i % 4)
            spot = list(at)
            spot.insert(AXES.index(a), coord[a])
            t = g[n][tuple(spot)].astype(F32)
            for d in range(3):
                t += r1[n][(d, *at)].astype(F32)
            s1[n][at] = t.astype(BF16)
            return _

        lax.fori_loop(0, 16, each, 0)
        b = order[1]
        for d in range(1, 4):
            send(
                s1[n].at[pick(rest, b, (coord[b] + d) % 4)], r2[n].at[d - 1],
                rs.at[n, 1], rr.at[n, 1], go[b](pos, d),
            )

    def sum_two(n):
        order = STREAMS[n][2]
        rest = [b for b in AXES if b != order[0]]
        settle(r2[n], rr.at[n, 1])
        settle(r2[n], rs.at[n, 1])
        b, c = order[1], order[2]
        for i in range(4):
            spot = [i]
            spot.insert(rest.index(b), coord[b])
            t = s1[n][tuple(spot)].astype(F32)
            for d in range(3):
                t += r2[n][d, i].astype(F32)
            s2[n][i] = t.astype(BF16)
        for d in range(1, 4):
            send(
                s2[n].at[(coord[c] + d) % 4], r3[n].at[d - 1],
                rs.at[n, 2], rr.at[n, 2], go[c](pos, d),
            )

    def sum_three(n):
        first, width, order = STREAMS[n]
        settle(r3[n], rr.at[n, 2])
        settle(r3[n], rs.at[n, 2])
        t = s2[n][coord[order[2]]].astype(F32)
        for d in range(3):
            t += r3[n][d].astype(F32)
        wgrad[:, pl.ds(first, width)] = t * (1.0 / math.sqrt(BLOCK * 128))

    def layer_tile(c, _):
        cols = pl.ds(pl.multiple_of(c * 256, 256), 256)
        layer[:, cols] = jnp.dot(
            att[...], wbuf[:, cols], preferred_element_type=F32
        ).astype(BF16)
        return _

    stores = [
        pltpu.make_async_copy(src, dst, outs.at[n])
        for n, (src, dst) in enumerate(
            ((grad_q, grad_q_out), (own_k, own_k_out), (own_v, own_v_out), (layer, layer_out))
        )
    ]
    for p in range(PARTS):
        return_y(p)
    each = HEADS // PARTS
    for p in range(PARTS):
        return_x(p)
        if p >= 1:
            return_z(p - 1)
        if p == 1:
            loads[7].wait()
            lax.fori_loop(0, 8, layer_tile, 0)
            stores[3].start()
        if p == LATE:
            partial(0)
            send_one(0)
        lax.fori_loop(p * each, (p + 1) * each, backward_own, 0, unroll=each)
        for level, step in enumerate((sum_one, sum_two)):
            for n in range(3):
                if WHEN[n][level] == p:
                    step(n)
    for store in stores[:3]:
        store.start()
    return_z(PARTS - 1)
    for n in (1, 2):
        sum_three(n)
    sum_two(0)
    sum_three(0)
    for p in range(PARTS):
        settle(back.at[p, pl.ds(4, 28)], zrs.at[p])
        settle(back.at[p, pl.ds(0, 4)], zsl.at[p])
        settle(zs.at[p, pl.ds(4, 28)], zss.at[p])
        settle(xb[p].at[pl.ds(1, 3)], xss.at[p])
        settle(ys.at[p], yss.at[p])
    settle(at_other, as_)
    for store in stores:
        store.wait()


def attend(tab, start, query, key, value, grad, landed, cot, cot_other, weight):
    slot = (ROWS, DH)
    tokens = (BLOCK, DIM)
    widths = [w for _, w, _ in STREAMS]
    per_stream = [
        [pltpu.VMEM((*lead, 16, w), BF16) for w in widths]
        for lead in ((4, 4, 4), (3, 4, 4), (4, 4), (3, 4), (4,), (3,))
    ]
    return pl.pallas_call(
        attend_kernel,
        out_shape=(
            jax.ShapeDtypeStruct((PARTS, 32, *slot), BF16),
            jax.ShapeDtypeStruct(tokens, BF16),
            jax.ShapeDtypeStruct((16, DIM), F32),
            jax.ShapeDtypeStruct(tokens, BF16),
            jax.ShapeDtypeStruct((HEADS, BLOCK, DH), BF16),
            jax.ShapeDtypeStruct((HEADS, BLOCK, DH), BF16),
        ),
        in_specs=[SMEM, SMEM, *[ANY] * 8],
        out_specs=(ANY, ANY, VMEM, ANY, ANY, ANY),
        scratch_shapes=[
            *[pltpu.VMEM((4, 4, 2, *slot), BF16)] * PARTS,
            *[pltpu.VMEM(tokens, BF16)] * 4,
            pltpu.VMEM((PARTS, 16, *slot), BF16),
            *[pltpu.VMEM(tokens, BF16)] * 2,
            pltpu.VMEM((DIM, DIM), BF16),
            pltpu.VMEM(tokens, BF16),
            pltpu.VMEM((HEADS, 4, 2, 16, BLOCK), BF16),
            pltpu.VMEM((HEADS, 4, 16, BLOCK), BF16),
            pltpu.VMEM((HEADS, 2, BLOCK, BLOCK), F32),
            pltpu.VMEM(tokens, BF16),
            pltpu.VMEM((HEADS, BLOCK, DH), BF16),
            pltpu.VMEM((HEADS, BLOCK, DH), BF16),
            pltpu.VMEM(tokens, BF16),
            pltpu.VMEM((PARTS, 16, *slot), BF16),
            pltpu.VMEM((PARTS, 12, *slot), BF16),
            pltpu.VMEM((PARTS, 4, 4, *slot), BF16),
            pltpu.VMEM((PARTS, 32, *slot), BF16),
            *[buf for level in per_stream for buf in level],
            *[pltpu.SemaphoreType.DMA((PARTS,))] * 7,
            *[pltpu.SemaphoreType.DMA] * 2,
            pltpu.SemaphoreType.DMA((8,)),
            pltpu.SemaphoreType.DMA((4,)),
            pltpu.SemaphoreType.DMA((3, 3)),
            pltpu.SemaphoreType.DMA((3, 3)),
        ],
        compiler_params=pltpu.CompilerParams(
            collective_id=1, has_side_effects=True, vmem_limit_bytes=62 << 20
        ),
        name="attend",
    )(tab, start, query, key, value, grad, landed, cot, cot_other, weight)


def final_kernel(
    tab, back_k, back_v, own_k, own_v, layer, grad_q, wgrad,
    grad_k, grad_v, layer_out, grad_q_out, wgrad_out, *sums
):
    layer_out[...] = layer[...]
    grad_q_out[...] = grad_q[...]
    wgrad_out[...] = wgrad[...]

    parts = [(back, own, i) for i in range(JOIN) for back, own in ((back_k, own_k), (back_v, own_v))]
    for total, (_, own, i) in zip(sums, parts):
        total[1:] = own[:, i * ROWS : (i + 1) * ROWS].astype(F32)

    def add(n, carry):
        h = tab[0, T_USED + n]
        for total, (back, _, i) in zip(sums, parts):
            total[h] += back[i, n].astype(F32)
        return carry

    lax.fori_loop(0, 32, add, 0, unroll=4)
    for h in range(HEADS):
        for total, (back, _, i) in zip(sums, parts):
            out = grad_k if back is back_k else grad_v
            out[i * ROWS : (i + 1) * ROWS, h * DH : (h + 1) * DH] = total[1 + h].astype(BF16)


def finish(tab, back, own_k, own_v, layer, grad_q, wgrad):
    steps = HALF // JOIN
    rows = pl.BlockSpec((ROWS * JOIN, DIM), lambda p, tab: (p, 0))
    own = pl.BlockSpec((HEADS, ROWS * JOIN, DH), lambda p, tab: (0, p, 0))
    whole = pl.BlockSpec((16, DIM), lambda p, tab: (0, 0))
    tokens = jax.ShapeDtypeStruct((BLOCK, DIM), BF16)
    return pl.pallas_call(
        final_kernel,
        out_shape=(tokens, tokens, tokens, tokens, jax.ShapeDtypeStruct((16, DIM), F32)),
        grid_spec=pltpu.PrefetchScalarGridSpec(
            num_scalar_prefetch=1,
            grid=(steps,),
            in_specs=[
                pl.BlockSpec((JOIN, 32, ROWS, DH), lambda p, tab: (p, 0, 0, 0)),
                pl.BlockSpec((JOIN, 32, ROWS, DH), lambda p, tab: (p + steps, 0, 0, 0)),
                own, own, rows, rows, whole,
            ],
            out_specs=[rows, rows, rows, rows, whole],
            scratch_shapes=[
                *[pltpu.VMEM((HEADS + 1, ROWS, DH), F32)] * (2 * JOIN),
            ],
        ),
        compiler_params=pltpu.CompilerParams(vmem_limit_bytes=60 << 20),
        name="finish",
    )(tab, back, back, own_k, own_v, layer, grad_q, wgrad)


def per_device(
    query_rows, key_rows, value_rows, cotangent, out_weight, sorted_blocks, window_start
):
    tab = make_tables(sorted_blocks)
    landed, grad, cot_other = fetch(tab, key_rows, value_rows, cotangent, out_weight)
    back, layer, wgrad, grad_q, own_k, own_v = attend(
        tab, window_start.reshape(1, HEADS), query_rows, key_rows, value_rows, grad, landed,
        cotangent, cot_other, out_weight,
    )
    grad_k, grad_v, layer, grad_q, wgrad = finish(
        tab, back, own_k, own_v, layer, grad_q, wgrad
    )
    return layer, grad_q, grad_k, grad_v, wgrad


def solution(mesh):
    rows = P(("sx", "sy"), None)
    return jax.shard_map(
        per_device,
        mesh=mesh,
        in_specs=(rows, rows, rows, rows, P(), P(), P(None, ("sx", "sy"))),
        out_specs=(rows, rows, rows, rows, rows),
        check_vma=False,
    )
```
